512 devices in a mesh: section: 2 (over core), fsdp: 64 (over z, y), tp: 4 (over x).
Axes of the slice: x: 4, y: 8, z: 8, core: 2. Of those that a mesh axis runs over, the one named last changes fastest.
Arguments:
- embeddings: bfloat16 [2, 8192, 8192], P(None, 'fsdp', 'tp'), may hold values from -80 to 80
- visual: bfloat16 [2, 64, 96, 8192], P('section', 'fsdp', None, 'tp'), may hold values from -80 to 80
- image_block_count: int32 [2, 64], P(None, 'fsdp'), may hold values from 1 to 3
- starts: int32 [2, 64], P(None, 'fsdp'), may hold values from 1 to 96, as said below
- lengths: int32 [2, 64], P(None, 'fsdp'), may hold values from 33 to 128
- queries: bfloat16 [2, 2, 8192, 8192], P('section', None, 'fsdp', 'tp'), may hold values from -100 to 100
- layer_key_vectors: bfloat16 [2, 2, 8192, 1024], P('section', None, 'fsdp', 'tp'), may hold values from -4.5 to 4.5
- input_norm_gain: bfloat16 [2, 8192], P('section', 'tp'), may hold values from 0.25 to 1.75
- frozen_value_weight: bfloat16 [2, 8192, 1024], P('section', 'tp', 'fsdp'), may hold values from -0.0625 to 0.0625
- adapter_down_map: bfloat16 [2, 8192, 16], P('section', 'tp'), may hold values from -0.0625 to 0.0625
- adapter_up_map: bfloat16 [2, 16, 1024], P('section'), may hold values from -1.5 to 1.5
- cotangent: bfloat16 [2, 8192, 8192], P(None, 'fsdp', 'tp'), may hold values from -6 to 6
Outputs:
- hidden_states: bfloat16 [2, 2, 8192, 8192], P('section', None, 'fsdp', 'tp')
- visual_grads: bfloat16 [2, 64, 96, 8192], P('section', 'fsdp', None, 'tp')
- down_map_gradient: float32 [2, 8192, 16], P('section', 'tp')
- up_map_gradient: float32 [2, 16, 1024], P('section', None, 'tp')
The draws below stay inside these ranges and needn't reach their ends.
Inputs may be any that keep to these rules, and one draw needn't show every extreme that they name: starts + 32 * image_block_count <= lengths for every sequence.
All inputs are finite; a program needn't handle non-finite values.
Results may differ from the reference program's by a relative error of at most 0.015.
Values may be sent and summed in bfloat16 or wider, within the bound.
No kernel may reach another device: no remote copies, remote signals or barrier semaphores. Data moves between devices by JAX's collectives and lax.ppermute only.
A program may use at most 64 MiB of HBM per device.

```python
import math
import jax
import jax.numpy as jnp
from jax import lax

MODEL_WIDTH = 8192
QH = 64
KVH = 8
HD = 128
ADAPTER_RANK = 16
SEQ = 128
MB = 2
TOKT = 32
MAXT = 3
VIS = 96
VALUE_WIDTH = 1024
LANGUAGE_LAYERS = 2
TOKENS = 8192
N_FSDP = 64


def scaled_field(key, base, low_scale, ramp_ratio):
    second, third = jax.random.split(key)
    shape = base.shape
    row_scale = jnp.exp(jax.random.uniform(second, shape[:-1] + (1,), jnp.float32, math.log(low_scale), math.log(3.0)))
    column = jnp.arange(shape[-1], dtype=jnp.float32) / (shape[-1] - 1)
    ramp = 2.0 * jnp.exp(math.log(ramp_ratio) * (column - 1.0))
    column_scale = jnp.exp(jax.random.uniform(third, (shape[-1],), jnp.float32, math.log(0.3), math.log(3.0))) * ramp
    return base * row_scale * column_scale


def field_draw(key, shape):
    first = jax.random.fold_in(key, 0)
    third = jax.random.fold_in(key, 2)
    base = jnp.clip(jax.random.normal(first, shape, jnp.float32), -4.0, 4.0)
    return scaled_field(third, base, 0.3, 16.0)


def draw_embeddings(key, part):
    key = jax.random.fold_in(key, 1)
    return field_draw(key, (MB, TOKENS, MODEL_WIDTH)).astype(jnp.bfloat16)


def draw_visual(key, part):
    key = jax.random.fold_in(key, 2)
    return field_draw(key, (MB, N_FSDP, VIS, MODEL_WIDTH)).astype(jnp.bfloat16)


def key_base(key):
    return jnp.clip(jax.random.normal(key, (LANGUAGE_LAYERS, MB, TOKENS, KVH * HD), jnp.float32), -4.0, 4.0)


def draw_layer_key_vectors(key, part):
    shared = key_base(key)
    return shared.astype(jnp.bfloat16)


def draw_queries(key, part):
    key = jax.random.fold_in(key, 4)
    fresh = jnp.clip(jax.random.normal(key, (LANGUAGE_LAYERS, MB, TOKENS, MODEL_WIDTH), jnp.float32), -4.0, 4.0)
    return fresh.astype(jnp.bfloat16)


def layout(key):
    first, second, third, fourth = jax.random.split(key, 4)
    total = MB * N_FSDP
    tiles = jax.random.randint(first, (MB, N_FSDP), 1, MAXT + 1)
    chosen_index = jax.random.randint(fourth, (), 0, total)
    index_grid = jnp.arange(total, dtype=jnp.int32).reshape(MB, N_FSDP)
    chosen = index_grid == chosen_index
    latest = index_grid == (chosen_index + 1) % total
    shortest = index_grid == (chosen_index + 2) % total
    tiles = jnp.where(chosen, MAXT, jnp.where(latest | shortest, 1, tiles))
    counts = tiles * TOKT
    seq_lengths = counts + 1 + jax.random.randint(second, (MB, N_FSDP), 0, SEQ - counts)
    seq_lengths = jnp.where(chosen | latest, SEQ, seq_lengths)
    seq_lengths = jnp.where(shortest, TOKT + 1, seq_lengths)
    begins = 1 + jax.random.randint(third, (MB, N_FSDP), 0, seq_lengths - counts)
    begins = jnp.where(latest, SEQ - TOKT, begins)
    begins = jnp.where(shortest, 1, begins)
    return (tiles.astype(jnp.int32), begins.astype(jnp.int32), seq_lengths.astype(jnp.int32))


def draw_image_block_count(key, part):
    shared = layout(key)
    return shared[0]


def draw_starts(key, part):
    shared = layout(key)
    return shared[1]


def draw_lengths(key, part):
    shared = layout(key)
    return shared[2]


def block_levels(own_key, dims, cuts, smallest, top_value):
    def one(axis_at, blocks):
        steps = jax.random.uniform(jax.random.fold_in(jax.random.fold_in(own_key, 6), axis_at), (blocks,), jnp.float32, smallest / len(cuts), top_value / len(cuts))
        return jnp.repeat(jnp.exp(steps), dims[axis_at] // blocks).reshape((-1,) + (1,) * (len(dims) - axis_at - 1))

    loudness = one(*cuts[0])
    for cut in cuts[1:]:
        loudness = loudness * one(*cut)
    return loudness


def normal_values(own_key, dims, spread, limit, shards=(), held_as=jnp.bfloat16):
    factor_of = block_levels(own_key, dims, shards, -0.22, 0.18) if shards else 1.0
    array = jax.random.normal(own_key, dims, jnp.float32) * spread * factor_of
    return jnp.minimum(jnp.maximum(array, -limit), limit).astype(held_as)


def setup_inputs(seed: int = 0) -> dict:
    seeds = jax.random.split(jax.random.key(seed), 13)
    embeddings = draw_embeddings(jax.random.fold_in(seeds[12], 71), 0)
    visual = draw_visual(jax.random.fold_in(seeds[12], 71), 0)
    image_block_count = draw_image_block_count(jax.random.fold_in(seeds[12], 71), 0)
    starts = draw_starts(jax.random.fold_in(seeds[12], 71), 0)
    lengths = draw_lengths(jax.random.fold_in(seeds[12], 71), 0)
    queries = draw_queries(jax.random.fold_in(seeds[12], 71), 0)
    layer_key_vectors = draw_layer_key_vectors(jax.random.fold_in(seeds[12], 71), 0)
    input_norm_gain = jnp.clip(1.0 + 0.15 * jax.random.normal(seeds[7], (LANGUAGE_LAYERS, MODEL_WIDTH), jnp.float32), 0.25, 1.75).astype(jnp.bfloat16)
    frozen_value_weight = normal_values(seeds[8], (LANGUAGE_LAYERS, MODEL_WIDTH, VALUE_WIDTH), MODEL_WIDTH ** -0.5, 0.0625, ((0, 2), (1, 4), (2, 64)))
    adapter_down_map = normal_values(seeds[9], (LANGUAGE_LAYERS, MODEL_WIDTH, ADAPTER_RANK), MODEL_WIDTH ** -0.5, 0.0625, ((0, 2), (1, 4)))
    adapter_up_map = normal_values(seeds[10], (LANGUAGE_LAYERS, ADAPTER_RANK, VALUE_WIDTH), ADAPTER_RANK ** -0.5, 1.5, ((0, 2),))
    cotangent = normal_values(seeds[11], (MB, TOKENS, MODEL_WIDTH), 1.0, 6.0, ((1, 64), (2, 4)))
    return {"embeddings": embeddings, "visual": visual, "image_block_count": image_block_count, "starts": starts, "lengths": lengths, "queries": queries, "layer_key_vectors": layer_key_vectors, "input_norm_gain": input_norm_gain, "frozen_value_weight": frozen_value_weight, "adapter_down_map": adapter_down_map, "adapter_up_map": adapter_up_map, "cotangent": cotangent}


ADAPTER_SCALE = 0.5
EPS = 1e-06
TOP_PRECISION = lax.Precision.HIGHEST

def product(left, right):
    return jnp.dot(left.astype(jnp.float32), right.astype(jnp.float32), precision=TOP_PRECISION)

def forward_over_sequence(hidden_input, query_matrix, key_matrix, sequence_length, norm_factor, frozen_value_weight, adapter_down_map, adapter_up_map):
    row_count = hidden_input.shape[0]
    in_float = hidden_input.astype(jnp.float32)
    inverse_norm = lax.rsqrt(lax.optimization_barrier(jnp.mean(in_float * in_float, axis=-1, keepdims=True)) + EPS)
    normalized_input = (in_float * inverse_norm * norm_factor.astype(jnp.float32)).astype(jnp.bfloat16)
    adapter_rows = product(normalized_input, adapter_down_map)
    frozen_values = product(normalized_input, frozen_value_weight)
    adapter_value_rows = product(adapter_rows, adapter_up_map)
    value_vectors = (frozen_values + ADAPTER_SCALE * adapter_value_rows).astype(jnp.bfloat16)
    per_group = QH // KVH
    query_heads = query_matrix.astype(jnp.float32).reshape(row_count, KVH, per_group, HD)
    key_heads = key_matrix.astype(jnp.float32).reshape(row_count, KVH, HD)
    scores = jnp.einsum('igkd,jgd->gkij', query_heads, key_heads) / math.sqrt(HD)
    positions = jnp.arange(row_count, dtype=jnp.int32)
    allowed = (positions[None, :] <= positions[:, None]) & (positions[None, :] < sequence_length)
    scores = jnp.where(allowed, scores, -jnp.inf)
    softmax_weights = jax.nn.softmax(scores, axis=-1).astype(jnp.bfloat16)
    value_heads = value_vectors.astype(jnp.float32).reshape(row_count, KVH, HD)
    attended = jnp.einsum('gkij,jgd->igkd', softmax_weights.astype(jnp.float32), value_heads).reshape(row_count, MODEL_WIDTH)
    final_result = (in_float + attended).astype(jnp.bfloat16)
    return (final_result, (normalized_input, inverse_norm, adapter_rows, softmax_weights))

def backward_over_sequence(output_gradient, hidden_input, query_matrix, key_matrix, sequence_length, norm_factor, frozen_value_weight, adapter_down_map, adapter_up_map):
    row_count = hidden_input.shape[0]
    ignored_value, saved_residuals = forward_over_sequence(hidden_input, query_matrix, key_matrix, sequence_length, norm_factor, frozen_value_weight, adapter_down_map, adapter_up_map)
    normalized_input, inverse_norm, adapter_rows, softmax_weights = saved_residuals
    per_group = QH // KVH
    grad_heads = output_gradient.astype(jnp.float32).reshape(row_count, KVH, per_group, HD)
    value_gradient = jnp.einsum('gkij,igkd->jgd', softmax_weights.astype(jnp.float32), grad_heads)
    value_gradient = value_gradient.reshape(row_count, KVH * HD).astype(jnp.bfloat16)
    adapter_gradient = ADAPTER_SCALE * product(value_gradient, adapter_up_map.T)
    normalized_gradient = product(value_gradient, frozen_value_weight.T)
    normalized_gradient = normalized_gradient + product(adapter_gradient, adapter_down_map.T)
    down_piece = product(normalized_input.T, adapter_gradient)
    up_piece = ADAPTER_SCALE * product(adapter_rows.T, value_gradient)
    in_float = hidden_input.astype(jnp.float32)
    scaled = normalized_gradient * norm_factor.astype(jnp.float32)
    dot_sums = lax.optimization_barrier(jnp.sum(scaled * in_float, axis=-1, keepdims=True))
    grad_in = inverse_norm * scaled - in_float * inverse_norm ** 3 * dot_sums / MODEL_WIDTH
    grad_total = (output_gradient.astype(jnp.float32) + grad_in).astype(jnp.bfloat16)
    return (grad_total, down_piece, up_piece)

def reference(embeddings, visual, image_block_count, starts, lengths, queries, layer_key_vectors, input_norm_gain, frozen_value_weight, adapter_down_map, adapter_up_map, cotangent):
    flat = MB * N_FSDP
    positions = jnp.arange(SEQ, dtype=jnp.int32)
    offsets = positions[None, None, :] - starts[:, :, None]
    inside = (offsets >= 0) & (offsets < image_block_count[:, :, None] * TOKT)
    clipped = jnp.clip(offsets, 0, VIS - 1).astype(jnp.int32)
    picked = jax.vmap(jax.vmap(lambda table, rows_at: table[rows_at]))(visual, clipped)
    text_rows = embeddings.reshape(MB, N_FSDP, SEQ, MODEL_WIDTH)
    entry = jnp.where(inside[..., None], picked, text_rows).reshape(flat, SEQ, MODEL_WIDTH)
    seq_lengths = lengths.reshape(flat)
    layer_inputs = []
    outputs = []
    current = entry
    for index_of_layer in range(LANGUAGE_LAYERS):
        layer_inputs.append(current)
        query_flat = queries[index_of_layer].reshape(flat, SEQ, MODEL_WIDTH)
        key_flat = layer_key_vectors[index_of_layer].reshape(flat, SEQ, VALUE_WIDTH)

        def run_one(packed, index_of_layer=index_of_layer):
            hidden_input, query_matrix, key_matrix, sequence_length = packed
            return forward_over_sequence(hidden_input, query_matrix, key_matrix, sequence_length, input_norm_gain[index_of_layer], frozen_value_weight[index_of_layer], adapter_down_map[index_of_layer], adapter_up_map[index_of_layer])[0]
        current = lax.map(run_one, (current, query_flat, key_flat, seq_lengths))
        outputs.append(current.reshape(MB, TOKENS, MODEL_WIDTH))
    factor = 1.0 / math.sqrt(MB * TOKENS)
    grad_rows = cotangent.reshape(flat, SEQ, MODEL_WIDTH)
    down_grads = [None] * LANGUAGE_LAYERS
    up_grads = [None] * LANGUAGE_LAYERS
    for index_of_layer in reversed(range(LANGUAGE_LAYERS)):
        query_flat = queries[index_of_layer].reshape(flat, SEQ, MODEL_WIDTH)
        key_flat = layer_key_vectors[index_of_layer].reshape(flat, SEQ, VALUE_WIDTH)

        def back_one(packed, index_of_layer=index_of_layer):
            output_gradient, hidden_input, query_matrix, key_matrix, sequence_length = packed
            return backward_over_sequence(output_gradient, hidden_input, query_matrix, key_matrix, sequence_length, input_norm_gain[index_of_layer], frozen_value_weight[index_of_layer], adapter_down_map[index_of_layer], adapter_up_map[index_of_layer])
        grad_rows, down_parts, up_parts = lax.map(back_one, (grad_rows, layer_inputs[index_of_layer], query_flat, key_flat, seq_lengths))
        down_grads[index_of_layer] = lax.optimization_barrier(jnp.sum(down_parts, axis=0)) * factor
        up_grads[index_of_layer] = lax.optimization_barrier(jnp.sum(up_parts, axis=0)) * factor
    entry_grad = grad_rows.reshape(MB, N_FSDP, SEQ, MODEL_WIDTH)
    slots = jnp.arange(VIS, dtype=jnp.int32)
    slot_rows = jnp.clip(starts[:, :, None] + slots[None, None, :], 0, SEQ - 1).astype(jnp.int32)
    slot_valid = slots[None, None, :] < image_block_count[:, :, None] * TOKT
    slot_grads = jax.vmap(jax.vmap(lambda table, rows_at: table[rows_at]))(entry_grad, slot_rows)
    visual_grads = jnp.where(slot_valid[..., None], slot_grads, jnp.zeros_like(slot_grads)).astype(jnp.bfloat16)
    return (jnp.stack(outputs), visual_grads, jnp.stack(down_grads), jnp.stack(up_grads))
```

```python
import functools
import math

import jax
import jax.numpy as jnp
from jax import lax
from jax.experimental import pallas as pl
from jax.experimental.pallas import tpu as pltpu
from jax.sharding import PartitionSpec as P

MODEL_WIDTH = 8192
HD = 128
TOKT = 32
ADAPTER_SCALE = 0.5
EPS = 1e-06

SEQ = 128
MB = 2
ROWS = MB * SEQ
VIS = 96
RANK = 16
HEADS = 8
HALF = HEADS * HD
KVH = 8
PEERS = 8
VMEM_BYTES = 40 * 1024 * 1024

BF = jnp.bfloat16
F32 = jnp.float32

R_VIS, R_Q, R_K, R_DN, R_UP, R_GN, R_END = 0, 96, 352, 384, 400, 416, 432
SMALL = 2 * RANK


def block_of(head):
    return (head % 2) * 4 + head // 2


def nt(left, right):
    return lax.dot_general(left, right, (((1,), (1,)), ((), ())), preferred_element_type=F32)


def tn(left, right):
    return lax.dot_general(left, right, (((0,), (0,)), ((), ())), preferred_element_type=F32)


def nn(left, right):
    return jnp.dot(left, right, preferred_element_type=F32)


def stack_heads(block):
    return jnp.concatenate([block[:, h * HD : (h + 1) * HD] for h in range(HEADS)], axis=0)


def unstack_heads(block):
    return jnp.concatenate([block[h * SEQ : (h + 1) * SEQ, :] for h in range(HEADS)], axis=1)


def columns_to_rows(*columns):
    lane = lax.broadcasted_iota(jnp.int32, (ROWS, HD), 1)
    square = jnp.zeros((ROWS, HD), F32)
    for at, column in enumerate(columns):
        square = jnp.where(lane == at, column, square)
    return square.T[:RANK, :]


def rows_to_columns(rows):
    padded = jnp.concatenate([rows, jnp.zeros((HD - RANK, ROWS), F32)], axis=0)
    return padded.T


def split_parts(rows):
    high = rows.astype(BF)
    low = (rows - high.astype(F32)).astype(BF)
    parts = [part[:, at : at + HD] for part in (high, low) for at in (0, HD)]
    return jnp.concatenate(parts, axis=0)


def join_parts(block, count):
    parts = [block[at * count : (at + 1) * count, :].astype(F32) for at in range(4)]
    return jnp.concatenate([parts[0] + parts[2], parts[1] + parts[3]], axis=1)


def inverse_of(squares):
    return lax.rsqrt(squares / MODEL_WIDTH + EPS)


def pack_kernel(core, visual, queries, keys, down, up, gain, out):
    other = 1 - core[0]
    at = pl.multiple_of(other * HALF, HALF)
    key_at = pl.multiple_of(other * HD, HD)
    out[R_VIS:R_Q, :] = visual[:, pl.ds(at, HALF)]
    out[R_Q:R_K, :] = queries[:, pl.ds(at, HALF)]
    for j in range(8):
        out[R_K:R_DN, j * HD : (j + 1) * HD] = keys[j * 32 : (j + 1) * 32, pl.ds(key_at, HD)]
    out[R_DN:R_UP, :] = down[:, pl.ds(at, HALF)]
    out[R_UP:R_GN, :] = up[...]
    out[R_GN:R_END, :] = gain[:, pl.ds(at, HALF)]


def softmax_of(query_rows, key_rows, length):
    scores = nt(stack_heads(query_rows), key_rows) / math.sqrt(HD)
    shape = scores.shape
    row = lax.rem(lax.broadcasted_iota(jnp.int32, shape, 0), SEQ)
    column = lax.broadcasted_iota(jnp.int32, shape, 1)
    allowed = (column <= row) & (column < length)
    scores = jnp.where(allowed, scores, -jnp.inf)
    top = jnp.max(scores, axis=-1, keepdims=True)
    weights = jnp.exp(scores - top)
    return (weights / jnp.sum(weights, axis=-1, keepdims=True)).astype(BF)


def prepare_kernel(
    core, counts, starts, lengths,
    received, visual, queries, keys, down, up, gain, embeddings, cotangent,
    weights, entry, cotangent_half, downs, ups, gains, payload,
):
    own = core[0]
    other = 1 - own
    at = pl.multiple_of(own * HALF, HALF)
    key_at = pl.multiple_of(own * HD, HD)
    half = pl.ds(at, HALF)
    downs[own] = down[:, half]
    downs[other] = received[R_DN:R_UP, :]
    ups[own] = up[...]
    ups[other] = received[R_UP:R_GN, :]
    gains[own] = gain[:, half]
    gains[other] = received[R_GN:R_END, :]
    position = lax.broadcasted_iota(jnp.int32, (SEQ, VIS), 0)
    slot = lax.broadcasted_iota(jnp.int32, (SEQ, VIS), 1)
    place = lax.broadcasted_iota(jnp.int32, (SEQ, 1), 0)
    for index, table in ((own, visual[:, half]), (other, received[R_VIS:R_Q, :])):
        begin = starts[index]
        count = counts[index] * TOKT
        placing = ((position == begin + slot) & (slot < count)).astype(F32).astype(BF)
        inserted = nn(placing, table).astype(BF)
        covered = (place >= begin) & (place < begin + count)
        rows = pl.ds(pl.multiple_of(index * SEQ, SEQ), SEQ)
        entry[rows, :] = jnp.where(covered, inserted, embeddings[index, :, half])
    for m in range(MB):
        rows = slice(m * SEQ, (m + 1) * SEQ)
        cotangent_half[rows, :] = cotangent[m, :, half]
        weights[own, m] = softmax_of(queries[rows, half], keys[rows, pl.ds(key_at, HD)], lengths[m])
        other_keys = jnp.concatenate(
            [received[R_K:R_DN, j * HD : (j + 1) * HD] for j in range(4 * m, 4 * m + 4)], axis=0
        )
        weights[other, m] = softmax_of(
            received[R_Q + m * SEQ : R_Q + (m + 1) * SEQ, :], other_keys, lengths[m]
        )
    value_gradient = jnp.concatenate(
        [
            tn(weights[1, m], stack_heads(cotangent_half[m * SEQ : (m + 1) * SEQ, :]))
            for m in range(MB)
        ],
        axis=0,
    ).astype(BF)
    entry_float = entry[...].astype(F32)
    squares = jnp.sum(entry_float * entry_float, axis=-1, keepdims=True)
    gained = (entry_float * gains[0][0:1, :].astype(F32)).astype(BF)
    small = jnp.concatenate([nt(downs[0], gained), columns_to_rows(squares)], axis=0)
    block = jnp.concatenate([value_gradient, split_parts(small)], axis=0)
    for peer in range(PEERS):
        payload[peer] = block


def entry_norm_kernel(
    received, entry, downs, ups, gains, normed, inverse, adapter_rows, full_gradient, lora_gradient
):
    total = jnp.zeros((SMALL, ROWS), F32)
    for peer in range(PEERS):
        total = total + join_parts(received[peer, ROWS:, :], SMALL)
    column = inverse_of(rows_to_columns(total[RANK:, :])[:, 0:1])
    inverse[...] = jnp.broadcast_to(column, (ROWS, HD))
    adapter_rows[...] = total[:RANK, :] * inverse_of(total[RANK : RANK + 1, :])
    gain = gains[0][0:1, :].astype(F32)
    normed[...] = (entry[...].astype(F32) * column * gain).astype(BF)
    for head in range(KVH):
        full_gradient[:, head * HD : (head + 1) * HD] = received[block_of(head), :ROWS, :]
    lora_gradient[...] = ADAPTER_SCALE * nt(ups[1], full_gradient[...])


def values_kernel(layer, normed, columns, downs, ups, out):
    rows = normed[...]
    adapter = (ADAPTER_SCALE * nt(rows, downs[layer])).astype(BF)
    for pair in range(KVH // 2):
        weight = columns[2 * pair : 2 * pair + 2, layer].reshape(2 * HD, HALF)
        up = ups[layer][:, 2 * pair * HD : (2 * pair + 2) * HD]
        partial = (nt(rows, weight) + nn(adapter, up)).astype(BF)
        out[block_of(2 * pair)] = partial[:, :HD]
        out[block_of(2 * pair + 1)] = partial[:, HD:]


def scaled_kernel(full_gradient, lora_gradient, columns, downs, gains, scaled):
    weight = columns[:, 1].reshape(KVH * HD, HALF)
    grad = nn(full_gradient[...], weight) + tn(lora_gradient[...].astype(BF), downs[1])
    scaled[...] = grad * gains[1][0:1, :].astype(F32)


def attended_rows(weights, layer, value_rows):
    return jnp.concatenate(
        [
            unstack_heads(nn(weights[layer, m], value_rows[m * SEQ : (m + 1) * SEQ, :]))
            for m in range(MB)
        ],
        axis=0,
    )


def first_output_kernel(
    received, weights, entry, scaled, downs, gains, hidden, value_rows, payload
):
    values = received[0].astype(F32)
    for peer in range(1, PEERS):
        values = values + received[peer].astype(F32)
    value_rows[...] = values
    attended = attended_rows(weights, 0, values.astype(BF))
    output = (entry[...].astype(F32) + attended).astype(BF)
    hidden[...] = output
    output_float = output.astype(F32)
    squares = jnp.sum(output_float * output_float, axis=-1, keepdims=True)
    dots = jnp.sum(output_float * scaled[...], axis=-1, keepdims=True)
    gained = (output_float * gains[1][0:1, :].astype(F32)).astype(BF)
    small = jnp.concatenate([nt(downs[1], gained), columns_to_rows(squares, dots)], axis=0)
    for peer in range(PEERS):
        payload[peer] = small


def first_gradient_kernel(
    received, weights, hidden, scaled, cotangent_half, gains, value_rows,
    gradient, normed, adapter_rows, payload,
):
    total = received[0]
    for peer in range(1, PEERS):
        total = total + received[peer]
    sums = rows_to_columns(total[RANK:, :])
    column = inverse_of(sums[:, 0:1])
    factor = column * column * column * sums[:, 1:2] / MODEL_WIDTH
    adapter_rows[...] = total[:RANK, :] * inverse_of(total[RANK : RANK + 1, :])
    hidden_float = hidden[...].astype(F32)
    gain = gains[1][0:1, :].astype(F32)
    normed[...] = (hidden_float * column * gain).astype(BF)
    grad = (
        cotangent_half[...].astype(F32) + column * scaled[...] - hidden_float * factor
    ).astype(BF)
    gradient[...] = grad
    value_gradient = jnp.concatenate(
        [tn(weights[0, m], stack_heads(grad[m * SEQ : (m + 1) * SEQ, :])) for m in range(MB)],
        axis=0,
    ).astype(BF)
    dots = jnp.sum(value_gradient.astype(F32) * value_rows[...], axis=-1, keepdims=True)
    block = jnp.concatenate([value_gradient, split_parts(columns_to_rows(dots))], axis=0)
    for peer in range(PEERS):
        payload[peer] = block


def map_chunks(down_gradient, up_gradient):
    quarter = HALF // 4
    left = jnp.concatenate(
        [down_gradient[:, q * quarter : (q + 1) * quarter] for q in range(4)], axis=0
    )
    right = jnp.concatenate([up_gradient, jnp.zeros((3 * RANK, HD), F32)], axis=0)
    return jnp.concatenate([left, right], axis=1)


def map_gradient_kernel(
    core, received, ups, normed_0, adapter_0, normed_1, adapter_1, full_gradient, lora_gradient_1,
    last_gradient, lora_gradient_0, out,
):
    own = core[0] * 4 + core[1]
    for head in range(KVH):
        last_gradient[:, head * HD : (head + 1) * HD] = received[block_of(head), :ROWS, :]
    lora_0 = ADAPTER_SCALE * nt(ups[0], last_gradient[...])
    lora_gradient_0[...] = lora_0
    down_0 = nn(lora_0.astype(BF), normed_0[...])
    up_0 = ADAPTER_SCALE * nn(adapter_0[...].astype(BF), received[own, :ROWS, :])
    out[0] = map_chunks(down_0, up_0)
    own_columns = pl.ds(pl.multiple_of((2 * core[1] + core[0]) * HD, HD), HD)
    down_1 = nn(lora_gradient_1[...].astype(BF), normed_1[...])
    up_1 = ADAPTER_SCALE * nn(adapter_1[...].astype(BF), full_gradient[:, own_columns])
    out[1] = map_chunks(down_1, up_1)


def slot_gradient_kernel(
    core, counts, starts,
    received, last_gradient, lora_gradient, columns, downs, gains, entry, inverse, gradient,
    slots,
):
    total = jnp.zeros((RANK, ROWS), F32)
    for peer in range(PEERS):
        total = total + join_parts(received[peer, ROWS:, :], RANK)
    column = inverse[:, 0:1]
    factor = column * column * rows_to_columns(total)[:, 0:1] / MODEL_WIDTH
    weight = columns[:, 0].reshape(KVH * HD, HALF)
    grad = nn(last_gradient[...], weight) + tn(lora_gradient[...].astype(BF), downs[0])
    scaled = grad * gains[0][0:1, :].astype(F32)
    rows = (
        gradient[...].astype(F32) + column * scaled - entry[...].astype(F32) * factor
    ).astype(BF)
    slot = lax.broadcasted_iota(jnp.int32, (VIS, SEQ), 0)
    position = lax.broadcasted_iota(jnp.int32, (VIS, SEQ), 1)
    for m in range(MB):
        picking = ((position == starts[m] + slot) & (slot < counts[m] * TOKT)).astype(F32).astype(BF)
        slots[m] = nn(picking, rows[m * SEQ : (m + 1) * SEQ, :]).astype(BF)


def second_output_kernel(values, weights, hidden, out):
    attended = attended_rows(weights, 1, values[...])
    out[...] = (hidden[...].astype(F32) + attended).astype(BF)


def call(kernel, name, shapes, scalars, arrays, flops=0):
    in_specs = [pl.BlockSpec(memory_space=pltpu.SMEM)] * len(scalars)
    in_specs += [pl.BlockSpec(memory_space=pltpu.VMEM)] * len(arrays)
    outs = [jax.ShapeDtypeStruct(shape, dtype) for shape, dtype in shapes]
    moved = sum(a.size * a.dtype.itemsize for a in arrays)
    moved += sum(math.prod(shape) * jnp.dtype(dtype).itemsize for shape, dtype in shapes)
    result = pl.pallas_call(
        kernel,
        out_shape=outs,
        in_specs=in_specs,
        out_specs=[pl.BlockSpec(memory_space=pltpu.VMEM)] * len(outs),
        compiler_params=pltpu.CompilerParams(vmem_limit_bytes=VMEM_BYTES),
        cost_estimate=pl.CostEstimate(flops=flops, bytes_accessed=moved, transcendentals=0),
        name=name,
    )(*scalars, *arrays)
    return result


def swap_cores(block):
    return lax.ppermute(block, "section", [(0, 1), (1, 0)])


def to_heads(block):
    return lax.all_to_all(block, ("section", "tp"), 0, 0)


def on_device(
    embeddings,
    visual,
    image_block_count,
    starts,
    lengths,
    queries,
    layer_key_vectors,
    input_norm_gain,
    frozen_value_weight,
    adapter_down_map,
    adapter_up_map,
    cotangent,
):
    section = lax.axis_index("section")
    tp = lax.axis_index("tp")
    n_fsdp = lax.axis_size("fsdp")
    n_y = n_fsdp // KVH
    core = jnp.stack([section, tp]).astype(jnp.int32)
    counts = image_block_count[:, 0]
    begins = starts[:, 0]
    seq_lengths = lengths[:, 0]

    shard = frozen_value_weight[0].T
    pieces = shard.reshape(shard.shape[0], 2, HALF).transpose(1, 0, 2)
    pieces = jnp.broadcast_to(pieces[:, None], (2, n_y) + pieces.shape[1:])
    pieces = pieces.reshape((2 * n_y,) + pieces.shape[2:])
    head_groups = [
        [s * n_fsdp + z * n_y + y for s in range(2) for y in range(n_y)] for z in range(KVH)
    ]
    head_columns = lax.all_to_all(
        pieces, ("section", "fsdp"), 0, 0, axis_index_groups=head_groups
    ).reshape(2, HD, HALF)
    row_groups = [[z * n_y + y for z in range(KVH)] for y in range(n_y)]
    columns = lax.all_gather(head_columns, "fsdp", axis=0, axis_index_groups=row_groups)

    own_visual = visual[0, 0]
    own_queries = queries[0].reshape(ROWS, 2 * HALF)
    own_keys = layer_key_vectors[0].reshape(ROWS, 2 * HD)
    own_down = adapter_down_map[0].T
    own_up = adapter_up_map[0]
    own_gain = jnp.broadcast_to(input_norm_gain, (RANK, 2 * HALF))
    own = (own_visual, own_queries, own_keys, own_down, own_up, own_gain)
    (packed,) = call(pack_kernel, "pack", [((R_END, HALF), BF)], (core,), own)
    received = swap_cores(packed)

    wide = ((ROWS, HALF), BF)
    small = ((RANK, ROWS), F32)
    maps = ((2, RANK, HALF), BF)
    weights, entry, cotangent_half, downs, ups, gains, payload = call(
        prepare_kernel,
        "prepare",
        [
            ((2, MB, HEADS * SEQ, SEQ), BF),
            wide,
            wide,
            maps,
            maps,
            maps,
            ((PEERS, ROWS + 4 * SMALL, HD), BF),
        ],
        (core, counts, begins, seq_lengths),
        (received, *own, embeddings, cotangent),
    )
    normed_0, inverse_0, adapter_0, full_gradient, lora_gradient_1 = call(
        entry_norm_kernel,
        "entry_norm",
        [wide, ((ROWS, HD), F32), small, wide, small],
        (),
        (to_heads(payload), entry, downs, ups, gains),
    )

    blocks = ((PEERS, ROWS, HD), BF)
    (partial_0,) = call(
        functools.partial(values_kernel, 0), "values_0", [blocks], (), (normed_0, columns, downs, ups)
    )
    (scaled_1,) = call(
        scaled_kernel,
        "scaled_1",
        [((ROWS, HALF), F32)],
        (),
        (full_gradient, lora_gradient_1, columns, downs, gains),
    )
    hidden_0, value_rows, payload = call(
        first_output_kernel,
        "first_output",
        [wide, ((ROWS, HD), F32), ((PEERS, SMALL, ROWS), F32)],
        (),
        (to_heads(partial_0), weights, entry, scaled_1, downs, gains),
    )
    gradient, normed_1, adapter_1, payload = call(
        first_gradient_kernel,
        "first_gradient",
        [wide, wide, small, ((PEERS, ROWS + 4 * RANK, HD), BF)],
        (),
        (to_heads(payload), weights, hidden_0, scaled_1, cotangent_half, gains, value_rows),
    )
    gathered = to_heads(payload)
    (partial_1,) = call(
        functools.partial(values_kernel, 1), "values_1", [blocks], (), (normed_1, columns, downs, ups)
    )
    values_1 = lax.psum_scatter(partial_1, ("section", "tp"), scatter_dimension=0)

    last_gradient, lora_gradient_0, chunks = call(
        map_gradient_kernel,
        "map_gradient",
        [wide, small, ((2, 4 * RANK, HALF // 4 + HD), F32)],
        (core,),
        (gathered, ups, normed_0, adapter_0, normed_1, adapter_1, full_gradient, lora_gradient_1),
    )
    width = HALF // 4 + HD
    arrived = lax.all_to_all(
        chunks.reshape(2 * n_fsdp, 1, width), ("section", "fsdp"), 0, 0
    ).reshape(2, n_fsdp, width)
    summed = jnp.sum(arrived, axis=1)
    everywhere = lax.all_to_all(
        jnp.broadcast_to(summed.reshape(1, 1, 2 * width), (n_fsdp, 1, 2 * width)), "fsdp", 0, 0
    ).reshape(4, RANK, 2, width)
    everywhere = everywhere * (1.0 / math.sqrt(MB * SEQ * n_fsdp))
    down_sum = (
        everywhere[..., : HALF // 4].transpose(1, 2, 0, 3).reshape(RANK, 2 * HALF).T
    )
    up_sum = everywhere[0, :, :, HALF // 4 :].reshape(RANK, 2 * HD)

    (slots,) = call(
        slot_gradient_kernel,
        "slot_gradient",
        [((MB, VIS, HALF), BF)],
        (core, counts, begins),
        (
            gathered,
            last_gradient,
            lora_gradient_0,
            columns,
            downs,
            gains,
            entry,
            inverse_0,
            gradient,
        ),
    )
    (hidden_1,) = call(
        second_output_kernel, "second_output", [wide], (), (values_1, weights, hidden_0)
    )

    first = section == 0

    def halves(mine, theirs):
        left = jnp.where(first, mine, theirs)
        right = jnp.where(first, theirs, mine)
        return jnp.concatenate([left, right], axis=-1)

    slot_rows = halves(
        jnp.where(first, slots[0], slots[1]), swap_cores(jnp.where(first, slots[1], slots[0]))
    )
    hidden = halves(
        jnp.where(first, hidden_0, hidden_1), swap_cores(jnp.where(first, hidden_1, hidden_0))
    )
    return (
        hidden.reshape(1, MB, SEQ, 2 * HALF),
        slot_rows[None, None],
        down_sum[None],
        up_sum[None],
    )


def solution(mesh):
    return jax.shard_map(
        on_device,
        mesh=mesh,
        in_specs=(
            P(None, "fsdp", "tp"),
            P("section", "fsdp", None, "tp"),
            P(None, "fsdp"),
            P(None, "fsdp"),
            P(None, "fsdp"),
            P("section", None, "fsdp", "tp"),
            P("section", None, "fsdp", "tp"),
            P("section", "tp"),
            P("section", "tp", "fsdp"),
            P("section", "tp", None),
            P("section", None, None),
            P(None, "fsdp", "tp"),
        ),
        out_specs=(
            P("section", None, "fsdp", "tp"),
            P("section", "fsdp", None, "tp"),
            P("section", "tp", None),
            P("section", None, "tp"),
        ),
        check_vma=False,
    )
```

```python
import functools
import math

import jax
import jax.numpy as jnp
from jax import lax
from jax.experimental import pallas as pl
from jax.experimental.pallas import tpu as pltpu
from jax.sharding import PartitionSpec as P

MODEL_WIDTH = 8192
HD = 128
TOKT = 32
ADAPTER_SCALE = 0.5
EPS = 1e-06

SEQ = 128
MB = 2
ROWS = MB * SEQ
VIS = 96
RANK = 16
HEADS = 8
HALF = HEADS * HD
KVH = 8
PEERS = 8
VMEM_BYTES = 60 * 1024 * 1024

BF = jnp.bfloat16
F32 = jnp.float32

R_VIS, R_Q, R_K, R_DN, R_UP, R_GN, R_END = 0, 96, 352, 384, 400, 416, 432
R_SUM, R_LOW, R_PAY = ROWS, ROWS + RANK, ROWS + RANK + 2 * RANK
SUBLANES = 8


def block_of(head):
    return (head % 2) * 4 + head // 2


def nt(left, right):
    return lax.dot_general(left, right, (((1,), (1,)), ((), ())), preferred_element_type=F32)


def tn(left, right):
    return lax.dot_general(left, right, (((0,), (0,)), ((), ())), preferred_element_type=F32)


def nn(left, right):
    return jnp.dot(left, right, preferred_element_type=F32)


def stack_heads(block):
    return jnp.concatenate([block[:, h * HD : (h + 1) * HD] for h in range(HEADS)], axis=0)


def unstack_heads(block):
    return jnp.concatenate([block[h * SEQ : (h + 1) * SEQ, :] for h in range(HEADS)], axis=1)


def columns_to_rows(*columns):
    lane = lax.broadcasted_iota(jnp.int32, (ROWS, HD), 1)
    square = jnp.zeros((ROWS, HD), F32)
    for at, column in enumerate(columns):
        square = jnp.where(lane == at, column, square)
    return square.T[:SUBLANES, :]


def rows_to_columns(rows):
    padded = jnp.concatenate([rows, jnp.zeros((HD - SUBLANES, ROWS), F32)], axis=0)
    return padded.T


def payload_block(values, column, low_rank):
    row = columns_to_rows(column)[0:1, :]
    high = row.astype(BF).astype(F32)
    low = row - high
    at = lax.broadcasted_iota(jnp.int32, (RANK, HD), 0)
    sums = jnp.zeros((RANK, HD), F32)
    for index, part in enumerate((high[:, :HD], high[:, HD:], low[:, :HD], low[:, HD:])):
        sums = jnp.where(at == index, part, sums)
    low_rank = low_rank.astype(BF)
    return jnp.concatenate(
        [values, sums.astype(BF), low_rank[:, :HD], low_rank[:, HD:]], axis=0
    )


def total_of_payloads(blocks):
    sums = blocks[0, R_SUM:R_LOW, :].astype(F32)
    low_rank = blocks[0, R_LOW:, :].astype(F32)
    for peer in range(1, PEERS):
        sums = sums + blocks[peer, R_SUM:R_LOW, :].astype(F32)
        low_rank = low_rank + blocks[peer, R_LOW:, :].astype(F32)
    left = sums[0:1, :] + sums[2:3, :]
    right = sums[1:2, :] + sums[3:4, :]
    row = jnp.concatenate([left, right], axis=1)
    at = lax.broadcasted_iota(jnp.int32, (SUBLANES, ROWS), 0)
    rows = jnp.where(at == 0, row, 0.0)
    return rows, jnp.concatenate([low_rank[:RANK, :], low_rank[RANK:, :]], axis=1)


def inverse_of(squares):
    return lax.rsqrt(squares / MODEL_WIDTH + EPS)


class Loaded:
    def __init__(self, buffer, copies):
        self.buffer, self.copies, self.done = buffer, copies, set()
        for copy in copies:
            copy.start()

    def __call__(self, part=None):
        for at in range(len(self.copies)) if part is None else (part,):
            if at not in self.done:
                self.copies[at].wait()
                self.done.add(at)
        return self.buffer


class Stored:
    def __init__(self, buffer, target, semaphores):
        self.buffer, self.target, self.semaphores, self.copies = buffer, target, semaphores, []

    def send(self, block=None):
        at = self.semaphores.at[len(self.copies)]
        pair = (self.buffer, self.target)
        if block is not None:
            pair = (self.buffer.at[block], self.target.at[block])
        copy = pltpu.make_async_copy(*pair, at)
        copy.start()
        self.copies.append(copy)

    def finish(self):
        if not self.copies:
            self.send()
        for copy in self.copies:
            copy.wait()


def whole(scalars, ref, buffer):
    return [(ref, buffer)]


def layer_of(layer):
    return lambda scalars, ref, buffer: [(ref.at[layer], buffer)]


def half_of(other, width, rank=2):
    def view(scalars, ref, buffer):
        core = scalars[0][0]
        core = 1 - core if other else core
        part = pl.ds(pl.multiple_of(core * width, width), width)
        return [((ref.at[:, part] if rank == 2 else ref.at[:, :, part]), buffer)]

    return view


def columns_of(layer):
    def view(scalars, ref, buffer):
        pairs = [pl.ds(2 * at, 2) for at in range(KVH // 2)]
        return [(ref.at[pair, layer], buffer.at[pair]) for pair in pairs]

    return view


def call(kernel, name, results, scalars, operands, after=()):
    operands = [o if isinstance(o, tuple) else (o, o.shape, whole) for o in operands]
    arrays = [o[0] for o in operands]
    n_scalars, n_arrays, n_after, n_results = len(scalars), len(arrays), len(after), len(results)
    most = KVH // 2

    def body(*refs):
        refs = list(refs)
        scalar_refs = [refs.pop(0) for _ in range(n_scalars)]
        array_refs = [refs.pop(0) for _ in range(n_arrays)]
        del refs[:n_after]
        targets = [refs.pop(0) for _ in range(n_results)]
        buffers = [refs.pop(0) for _ in range(n_arrays)]
        out_buffers = [refs.pop(0) for _ in range(n_results)]
        in_semaphores, out_semaphores = refs
        loads = []
        for at, ref in enumerate(array_refs):
            pairs = operands[at][2](scalar_refs, ref, buffers[at])
            copies = [
                pltpu.make_async_copy(*pair, in_semaphores.at[at * most + k])
                for k, pair in enumerate(pairs)
            ]
            loads.append(Loaded(buffers[at], copies))
        stores = [
            Stored(out_buffers[at], targets[at], out_semaphores.at[at]) for at in range(n_results)
        ]
        kernel(*scalar_refs, *loads, *stores)
        for load in loads:
            load()
        for store in stores:
            store.finish()

    moved = sum(math.prod(o[1]) * o[0].dtype.itemsize for o in operands)
    moved += sum(math.prod(shape) * jnp.dtype(dtype).itemsize for shape, dtype in results)
    anywhere = pl.BlockSpec(memory_space=pltpu.HBM)
    return pl.pallas_call(
        body,
        out_shape=[jax.ShapeDtypeStruct(shape, dtype) for shape, dtype in results],
        in_specs=[pl.BlockSpec(memory_space=pltpu.SMEM)] * n_scalars
        + [anywhere] * (n_arrays + n_after),
        out_specs=[anywhere] * n_results,
        scratch_shapes=[pltpu.VMEM(o[1], o[0].dtype) for o in operands]
        + [pltpu.VMEM(shape, dtype) for shape, dtype in results]
        + [
            pltpu.SemaphoreType.DMA((n_arrays * most,)),
            pltpu.SemaphoreType.DMA((n_results, PEERS)),
        ],
        compiler_params=pltpu.CompilerParams(vmem_limit_bytes=VMEM_BYTES),
        cost_estimate=pl.CostEstimate(flops=0, bytes_accessed=moved, transcendentals=0),
        name=name,
    )(*scalars, *arrays, *after)


def send_to_all(payload, block):
    for peer in range(PEERS):
        payload.buffer[peer] = block
    payload.send()


def pack_kernel(core, visual, queries, keys, down, up, gain, packed):
    out = packed.buffer
    out[R_DN:R_UP, :] = down()[...]
    out[R_UP:R_GN, :] = up()[...]
    out[R_GN:R_END, :] = gain()[...]
    for j in range(8):
        out[R_K:R_DN, j * HD : (j + 1) * HD] = keys()[j * 32 : (j + 1) * 32, :]
    out[R_VIS:R_Q, :] = visual()[...]
    out[R_Q:R_K, :] = queries()[...]


def softmax_of(query_rows, key_rows, length):
    scores = nt(stack_heads(query_rows), key_rows) / math.sqrt(HD)
    shape = scores.shape
    row = lax.rem(lax.broadcasted_iota(jnp.int32, shape, 0), SEQ)
    column = lax.broadcasted_iota(jnp.int32, shape, 1)
    allowed = (column <= row) & (column < length)
    scores = jnp.where(allowed, scores, -jnp.inf)
    top = jnp.max(scores, axis=-1, keepdims=True)
    weights = jnp.exp(scores - top)
    return (weights / jnp.sum(weights, axis=-1, keepdims=True)).astype(BF)


def prepare_kernel(
    core, counts, starts, lengths,
    received, visual, queries, keys, down, up, gain, embeddings, cotangent,
    weights, entry, cotangent_half, downs, ups, gains, payload,
):
    own = core[0]
    other = 1 - own
    got = received()
    downs.buffer[own] = down()[...]
    downs.buffer[other] = got[R_DN:R_UP, :]
    ups.buffer[own] = up()[...]
    ups.buffer[other] = got[R_UP:R_GN, :]
    gains.buffer[own] = gain()[...]
    gains.buffer[other] = got[R_GN:R_END, :]
    for small in (downs, ups, gains):
        small.send()
    position = lax.broadcasted_iota(jnp.int32, (SEQ, VIS), 0)
    slot = lax.broadcasted_iota(jnp.int32, (SEQ, VIS), 1)
    place = lax.broadcasted_iota(jnp.int32, (SEQ, 1), 0)
    for index, table in ((own, visual()[...]), (other, got[R_VIS:R_Q, :])):
        begin = starts[index]
        count = counts[index] * TOKT
        placing = ((position == begin + slot) & (slot < count)).astype(F32).astype(BF)
        inserted = nn(placing, table).astype(BF)
        covered = (place >= begin) & (place < begin + count)
        rows = pl.ds(pl.multiple_of(index * SEQ, SEQ), SEQ)
        entry.buffer[rows, :] = jnp.where(covered, inserted, embeddings()[index])
    entry.send()
    for m in range(MB):
        rows = slice(m * SEQ, (m + 1) * SEQ)
        cotangent_half.buffer[rows, :] = cotangent()[m]
        weights.buffer[own, m] = softmax_of(queries()[rows, :], keys()[rows, :], lengths[m])
        other_keys = jnp.concatenate(
            [got[R_K:R_DN, j * HD : (j + 1) * HD] for j in range(4 * m, 4 * m + 4)], axis=0
        )
        weights.buffer[other, m] = softmax_of(
            got[R_Q + m * SEQ : R_Q + (m + 1) * SEQ, :], other_keys, lengths[m]
        )
    cotangent_half.send()
    weights.send()
    value_gradient = jnp.concatenate(
        [tn(weights.buffer[1, m], stack_heads(cotangent()[m])) for m in range(MB)], axis=0
    ).astype(BF)
    entry_float = entry.buffer[...].astype(F32)
    squares = jnp.sum(entry_float * entry_float, axis=-1, keepdims=True)
    gained = (entry_float * gains.buffer[0][0:1, :].astype(F32)).astype(BF)
    send_to_all(payload, payload_block(value_gradient, squares, nt(downs.buffer[0], gained)))


def entry_norm_kernel(
    received, entry, ups, gains, normed, inverse, adapter_rows, full_gradient, lora_gradient
):
    got = received()
    rows, low_rank = total_of_payloads(got)
    column = inverse_of(rows_to_columns(rows)[:, 0:1])
    inverse.buffer[...] = jnp.broadcast_to(column, (ROWS, HD))
    adapter_rows.buffer[...] = low_rank * inverse_of(rows[0:1, :])
    gain = gains()[0:1, :].astype(F32)
    normed.buffer[...] = (entry()[...].astype(F32) * column * gain).astype(BF)
    for head in range(KVH):
        full_gradient.buffer[:, head * HD : (head + 1) * HD] = got[block_of(head), :ROWS, :]
    lora_gradient.buffer[...] = ADAPTER_SCALE * nt(ups()[...], full_gradient.buffer[...])


def values_kernel(normed, downs, ups, columns, out):
    rows = normed()[...]
    adapter = (ADAPTER_SCALE * nt(rows, downs()[...])).astype(BF)
    ups()
    for pair in range(KVH // 2):
        weight = columns(pair)[2 * pair : 2 * pair + 2].reshape(2 * HD, HALF)
        up = ups()[:, 2 * pair * HD : (2 * pair + 2) * HD]
        partial = (nt(rows, weight) + nn(adapter, up)).astype(BF)
        for at in range(2):
            block = block_of(2 * pair + at)
            out.buffer[block] = partial[:, at * HD : (at + 1) * HD]
            out.send(block)


def weighted_gradient(full_gradient, lora_gradient, downs, gains, columns):
    grad = tn(lora_gradient.astype(BF), downs()[...])
    for pair in range(KVH // 2):
        weight = columns(pair)[2 * pair : 2 * pair + 2].reshape(2 * HD, HALF)
        grad = grad + nn(full_gradient[:, 2 * pair * HD : (2 * pair + 2) * HD], weight)
    return grad * gains()[0:1, :].astype(F32)


def scaled_kernel(full_gradient, lora_gradient, downs, gains, columns, scaled):
    scaled.buffer[...] = weighted_gradient(
        full_gradient()[...], lora_gradient()[...], downs, gains, columns
    )


def attended_rows(weights, value_rows):
    return jnp.concatenate(
        [
            unstack_heads(nn(weights[m], value_rows[m * SEQ : (m + 1) * SEQ, :]))
            for m in range(MB)
        ],
        axis=0,
    )


def first_output_kernel(received, weights, entry, scaled, hidden, value_rows, payload):
    got = received()
    values = got[0].astype(F32)
    for peer in range(1, PEERS):
        values = values + got[peer].astype(F32)
    value_rows.buffer[...] = values
    value_rows.send()
    attended = attended_rows(weights(), values.astype(BF))
    output = (entry()[...].astype(F32) + attended).astype(BF)
    hidden.buffer[...] = output
    hidden.send()
    output_float = output.astype(F32)
    squares = jnp.sum(output_float * output_float, axis=-1, keepdims=True)
    dots = jnp.sum(output_float * scaled()[...], axis=-1, keepdims=True)
    send_to_all(payload, columns_to_rows(squares, dots))


def first_gradient_kernel(
    received, hidden, scaled, cotangent_half, weights, value_rows, gains, downs,
    gradient, normed, inverse_row, payload,
):
    got = received()
    total = got[0]
    for peer in range(1, PEERS):
        total = total + got[peer]
    sums = rows_to_columns(total)
    column = inverse_of(sums[:, 0:1])
    factor = column * column * column * sums[:, 1:2] / MODEL_WIDTH
    inverse_row.buffer[...] = inverse_of(total)
    hidden_float = hidden()[...].astype(F32)
    grad = (
        cotangent_half()[...].astype(F32) + column * scaled()[...] - hidden_float * factor
    ).astype(BF)
    gradient.buffer[...] = grad
    gradient.send()
    gained = hidden_float * gains()[0:1, :].astype(F32)
    low_rank = nt(downs()[...], gained.astype(BF))
    value_gradient = jnp.concatenate(
        [tn(weights()[m], stack_heads(grad[m * SEQ : (m + 1) * SEQ, :])) for m in range(MB)],
        axis=0,
    ).astype(BF)
    dots = jnp.sum(value_gradient.astype(F32) * value_rows()[...], axis=-1, keepdims=True)
    send_to_all(payload, payload_block(value_gradient, dots, low_rank))
    normed.buffer[...] = (gained * column).astype(BF)


def map_chunks(down_gradient, up_gradient):
    quarter = HALF // 4
    left = jnp.concatenate(
        [down_gradient[:, q * quarter : (q + 1) * quarter] for q in range(4)], axis=0
    )
    right = jnp.concatenate([up_gradient, jnp.zeros((3 * RANK, HD), F32)], axis=0)
    return jnp.concatenate([left, right], axis=1)


def map_gradient_kernel(
    core, received, ups, normed_0, adapter_0, normed_1, inverse_row, gradient_1, lora_gradient_1,
    last_gradient, lora_gradient_0, column_sum, out,
):
    own = core[0] * 4 + core[1]
    got = received()
    for head in range(KVH):
        last_gradient.buffer[:, head * HD : (head + 1) * HD] = got[block_of(head), :ROWS, :]
    last_gradient.send()
    rows, low_rank = total_of_payloads(got)
    column_sum.buffer[...] = rows_to_columns(rows)
    lora_0 = ADAPTER_SCALE * nt(ups()[...], last_gradient.buffer[...])
    lora_gradient_0.buffer[...] = lora_0
    down_0 = nn(lora_0.astype(BF), normed_0()[...])
    up_0 = ADAPTER_SCALE * nn(adapter_0()[...].astype(BF), got[own, :ROWS, :])
    out.buffer[0] = map_chunks(down_0, up_0)
    down_1 = nn(lora_gradient_1()[...].astype(BF), normed_1()[...])
    adapter_1 = (low_rank * inverse_row()[0:1, :]).astype(BF)
    up_1 = ADAPTER_SCALE * nn(adapter_1, gradient_1()[...])
    out.buffer[1] = map_chunks(down_1, up_1)


def slot_gradient_kernel(
    counts, starts,
    last_gradient, lora_gradient, downs, gains, columns, entry, inverse, gradient, column_sum,
    slots,
):
    scaled = weighted_gradient(last_gradient()[...], lora_gradient()[...], downs, gains, columns)
    column = inverse()[:, 0:1]
    factor = column * column * column_sum()[:, 0:1] / MODEL_WIDTH
    rows = (
        gradient()[...].astype(F32) + column * scaled - entry()[...].astype(F32) * factor
    ).astype(BF)
    slot = lax.broadcasted_iota(jnp.int32, (VIS, SEQ), 0)
    position = lax.broadcasted_iota(jnp.int32, (VIS, SEQ), 1)
    for m in range(MB):
        picking = ((position == starts[m] + slot) & (slot < counts[m] * TOKT)).astype(F32).astype(BF)
        slots.buffer[m] = nn(picking, rows[m * SEQ : (m + 1) * SEQ, :]).astype(BF)


def second_output_kernel(values, weights, hidden, out):
    attended = attended_rows(weights(), values()[...])
    out.buffer[...] = (hidden()[...].astype(F32) + attended).astype(BF)


def maps_kernel(arrived, down_sum, up_sum, *, scale):
    rows = arrived()[...].reshape(4 * RANK, 2 * (HALF // 4 + HD)) * scale
    quarter, width = HALF // 4, HALF // 4 + HD
    for half in range(2):
        for q in range(4):
            to = half * HALF + q * quarter
            down_sum.buffer[:, to : to + quarter] = rows[
                q * RANK : (q + 1) * RANK, half * width : half * width + quarter
            ]
        up_sum.buffer[:, half * HD : (half + 1) * HD] = rows[
            :RANK, half * width + quarter : (half + 1) * width
        ]


def swap_cores(block):
    return lax.ppermute(block, "section", [(0, 1), (1, 0)])


def to_heads(block):
    return lax.all_to_all(block, ("section", "tp"), 0, 0)


def on_device(
    embeddings,
    visual,
    image_block_count,
    starts,
    lengths,
    queries,
    layer_key_vectors,
    input_norm_gain,
    frozen_value_weight,
    adapter_down_map,
    adapter_up_map,
    cotangent,
):
    section = lax.axis_index("section")
    tp = lax.axis_index("tp")
    n_fsdp = lax.axis_size("fsdp")
    n_y = n_fsdp // KVH
    core = jnp.stack([section, tp]).astype(jnp.int32)
    counts = image_block_count[:, 0]
    begins = starts[:, 0]
    seq_lengths = lengths[:, 0]

    shard = frozen_value_weight[0].T
    pieces = shard.reshape(shard.shape[0], 2, HALF).transpose(1, 0, 2)
    pieces = jnp.broadcast_to(pieces[:, None], (2, n_y) + pieces.shape[1:])
    pieces = pieces.reshape((2 * n_y,) + pieces.shape[2:])
    head_groups = [
        [s * n_fsdp + z * n_y + y for s in range(2) for y in range(n_y)] for z in range(KVH)
    ]
    head_columns = lax.all_to_all(
        pieces, ("section", "fsdp"), 0, 0, axis_index_groups=head_groups
    ).reshape(2, HD, HALF)
    row_groups = [[z * n_y + y for z in range(KVH)] for y in range(n_y)]
    columns = lax.all_gather(head_columns, "fsdp", axis=0, axis_index_groups=row_groups)

    def own(other):
        return (
            (visual[0, 0], (VIS, HALF), half_of(other, HALF)),
            (queries[0].reshape(ROWS, 2 * HALF), (ROWS, HALF), half_of(other, HALF)),
            (layer_key_vectors[0].reshape(ROWS, 2 * HD), (ROWS, HD), half_of(other, HD)),
            (adapter_down_map[0].T, (RANK, HALF), half_of(other, HALF)),
            adapter_up_map[0],
            (gain_rows, (RANK, HALF), half_of(other, HALF)),
        )

    gain_rows = jnp.broadcast_to(input_norm_gain, (RANK, 2 * HALF))
    (packed,) = call(pack_kernel, "pack", [((R_END, HALF), BF)], (core,), own(True))

    wide = ((ROWS, HALF), BF)
    low = ((RANK, ROWS), F32)
    lanes = ((ROWS, HD), F32)
    maps = ((2, RANK, HALF), BF)
    blocks = ((PEERS, ROWS, HD), BF)
    mixed = ((PEERS, R_PAY, HD), BF)
    half_rows = ((MB, SEQ, HALF), half_of(False, HALF, 3))
    weights, entry, cotangent_half, downs, ups, gains, payload = call(
        prepare_kernel,
        "prepare",
        [((2, MB, HEADS * SEQ, SEQ), BF), wide, wide, maps, maps, maps, mixed],
        (core, counts, begins, seq_lengths),
        (swap_cores(packed), *own(False), (embeddings, *half_rows), (cotangent, *half_rows)),
    )

    def at(layer, array):
        return (array, array.shape[1:], layer_of(layer))

    def weight_of(layer):
        return (columns, (KVH, HD, HALF), columns_of(layer))

    normed_0, inverse_0, adapter_0, gradient_values_1, lora_gradient_1 = call(
        entry_norm_kernel,
        "entry_norm",
        [wide, lanes, low, wide, low],
        (),
        (to_heads(payload), entry, at(1, ups), at(0, gains)),
    )
    (partial_0,) = call(
        values_kernel, "values_0", [blocks], (), (normed_0, at(0, downs), at(0, ups), weight_of(0))
    )
    (scaled_1,) = call(
        scaled_kernel,
        "scaled_1",
        [((ROWS, HALF), F32)],
        (),
        (gradient_values_1, lora_gradient_1, at(1, downs), at(1, gains), weight_of(1)),
    )
    hidden_0, value_rows, payload = call(
        first_output_kernel,
        "first_output",
        [wide, lanes, ((PEERS, SUBLANES, ROWS), F32)],
        (),
        (to_heads(partial_0), at(0, weights), entry, scaled_1),
    )
    gradient, normed_1, inverse_row, payload = call(
        first_gradient_kernel,
        "first_gradient",
        [wide, wide, ((SUBLANES, ROWS), F32), mixed],
        (),
        (
            to_heads(payload),
            hidden_0,
            scaled_1,
            cotangent_half,
            at(0, weights),
            value_rows,
            at(1, gains),
            at(1, downs),
        ),
    )
    gathered = to_heads(payload)
    (partial_1,) = call(
        values_kernel, "values_1", [blocks], (), (normed_1, at(1, downs), at(1, ups), weight_of(1))
    )
    values_1 = lax.psum_scatter(partial_1, ("section", "tp"), scatter_dimension=0)

    def own_columns(scalars, ref, buffer):
        head = 2 * scalars[0][1] + scalars[0][0]
        return [(ref.at[:, pl.ds(pl.multiple_of(head * HD, HD), HD)], buffer)]

    width = HALF // 4 + HD
    last_gradient, lora_gradient_0, column_sum, chunks = call(
        map_gradient_kernel,
        "map_gradient",
        [wide, low, lanes, ((2, 4 * RANK, width), F32)],
        (core,),
        (
            gathered,
            at(0, ups),
            normed_0,
            adapter_0,
            normed_1,
            inverse_row,
            (gradient_values_1, (ROWS, HD), own_columns),
            lora_gradient_1,
        ),
    )
    arrived = lax.all_to_all(
        chunks.reshape(2 * n_fsdp, 1, width), ("section", "fsdp"), 0, 0
    ).reshape(2, n_fsdp, width)
    summed = jnp.sum(arrived, axis=1).reshape(1, 1, 2 * width)
    everywhere = lax.all_to_all(
        jnp.broadcast_to(summed, (n_fsdp, 1, 2 * width)), "fsdp", 0, 0
    )
    down_sum, up_sum = call(
        functools.partial(maps_kernel, scale=1.0 / math.sqrt(MB * SEQ * n_fsdp)),
        "maps",
        [((RANK, 2 * HALF), F32), ((RANK, 2 * HD), F32)],
        (),
        (everywhere,),
    )

    (slots,) = call(
        slot_gradient_kernel,
        "slot_gradient",
        [((MB, VIS, HALF), BF)],
        (counts, begins),
        (
            last_gradient,
            lora_gradient_0,
            at(0, downs),
            at(0, gains),
            weight_of(0),
            entry,
            inverse_0,
            gradient,
            column_sum,
        ),
        after=(summed,),
    )
    (hidden_1,) = call(
        second_output_kernel,
        "second_output",
        [wide],
        (),
        (values_1, at(1, weights), hidden_0),
        after=(summed,),
    )

    first = section == 0

    def halves(mine, theirs):
        left = jnp.where(first, mine, theirs)
        right = jnp.where(first, theirs, mine)
        return jnp.concatenate([left, right], axis=-1)

    slot_rows = halves(
        jnp.where(first, slots[0], slots[1]), swap_cores(jnp.where(first, slots[1], slots[0]))
    )
    hidden = halves(
        jnp.where(first, hidden_0, hidden_1), swap_cores(jnp.where(first, hidden_1, hidden_0))
    )
    return (
        hidden.reshape(1, MB, SEQ, 2 * HALF),
        slot_rows[None, None],
        down_sum.T[None],
        up_sum[None],
    )


def solution(mesh):
    return jax.shard_map(
        on_device,
        mesh=mesh,
        in_specs=(
            P(None, "fsdp", "tp"),
            P("section", "fsdp", None, "tp"),
            P(None, "fsdp"),
            P(None, "fsdp"),
            P(None, "fsdp"),
            P("section", None, "fsdp", "tp"),
            P("section", None, "fsdp", "tp"),
            P("section", "tp"),
            P("section", "tp", "fsdp"),
            P("section", "tp", None),
            P("section", None, None),
            P(None, "fsdp", "tp"),
        ),
        out_specs=(
            P("section", None, "fsdp", "tp"),
            P("section", "fsdp", None, "tp"),
            P("section", "tp", None),
            P("section", None, "tp"),
        ),
        check_vma=False,
    )
```

```python
import functools
import math

import jax
import jax.numpy as jnp
from jax import lax
from jax.experimental import pallas as pl
from jax.experimental.pallas import tpu as pltpu
from jax.sharding import PartitionSpec as P

MODEL_WIDTH = 8192
HD = 128
TOKT = 32
ADAPTER_SCALE = 0.5
EPS = 1e-06

SEQ = 128
MB = 2
ROWS = MB * SEQ
VIS = 96
RANK = 16
HEADS = 8
HALF = HEADS * HD
KVH = 8
PEERS = 8
VMEM_BYTES = 40 * 1024 * 1024

BF = jnp.bfloat16
F32 = jnp.float32

R_VIS, R_Q, R_K, R_DN, R_UP, R_GN, R_END = 0, 96, 352, 384, 400, 416, 432
R_SUM, R_LOW, R_PAY = ROWS, ROWS + RANK, ROWS + RANK + 2 * RANK
SUBLANES = 8
M_ROWS = RANK + SUBLANES


def block_of(head):
    return (head % 2) * 4 + head // 2


def nt(left, right):
    return lax.dot_general(left, right, (((1,), (1,)), ((), ())), preferred_element_type=F32)


def tn(left, right):
    return lax.dot_general(left, right, (((0,), (0,)), ((), ())), preferred_element_type=F32)


def nn(left, right):
    return jnp.dot(left, right, preferred_element_type=F32)


def stack_heads(block):
    return jnp.concatenate([block[:, h * HD : (h + 1) * HD] for h in range(HEADS)], axis=0)


def unstack_heads(block):
    return jnp.concatenate([block[h * SEQ : (h + 1) * SEQ, :] for h in range(HEADS)], axis=1)


def columns_to_rows(*columns):
    lane = lax.broadcasted_iota(jnp.int32, (ROWS, HD), 1)
    square = jnp.zeros((ROWS, HD), F32)
    for at, column in enumerate(columns):
        square = jnp.where(lane == at, column, square)
    return square.T[:SUBLANES, :]


def rows_to_columns(rows):
    padded = jnp.concatenate([rows, jnp.zeros((HD - SUBLANES, ROWS), F32)], axis=0)
    return padded.T


def payload_block(values, column, low_rank):
    row = columns_to_rows(column)[0:1, :]
    high = row.astype(BF).astype(F32)
    low = row - high
    at = lax.broadcasted_iota(jnp.int32, (RANK, HD), 0)
    sums = jnp.zeros((RANK, HD), F32)
    for index, part in enumerate((high[:, :HD], high[:, HD:], low[:, :HD], low[:, HD:])):
        sums = jnp.where(at == index, part, sums)
    low_rank = low_rank.astype(BF)
    return jnp.concatenate(
        [values, sums.astype(BF), low_rank[:, :HD], low_rank[:, HD:]], axis=0
    )


def total_of_payloads(blocks):
    sums = blocks[0, R_SUM:R_LOW, :].astype(F32)
    low_rank = blocks[0, R_LOW:, :].astype(F32)
    for peer in range(1, PEERS):
        sums = sums + blocks[peer, R_SUM:R_LOW, :].astype(F32)
        low_rank = low_rank + blocks[peer, R_LOW:, :].astype(F32)
    left = sums[0:1, :] + sums[2:3, :]
    right = sums[1:2, :] + sums[3:4, :]
    row = jnp.concatenate([left, right], axis=1)
    at = lax.broadcasted_iota(jnp.int32, (SUBLANES, ROWS), 0)
    rows = jnp.where(at == 0, row, 0.0)
    return rows, jnp.concatenate([low_rank[:RANK, :], low_rank[RANK:, :]], axis=1)


def inverse_of(squares):
    return lax.rsqrt(squares / MODEL_WIDTH + EPS)


class Loaded:
    def __init__(self, buffer, copies):
        self.buffer, self.copies, self.done = buffer, copies, set()
        for copy in copies:
            copy.start()

    def __call__(self, part=None):
        for at in range(len(self.copies)) if part is None else (part,):
            if at not in self.done:
                self.copies[at].wait()
                self.done.add(at)
        return self.buffer


class Stored:
    def __init__(self, buffer, target, semaphores):
        self.buffer, self.target, self.semaphores, self.copies = buffer, target, semaphores, []

    def send(self, repeated=False):
        targets = [self.target.at[peer] for peer in range(PEERS)] if repeated else [self.target]
        for at, target in enumerate(targets):
            copy = pltpu.make_async_copy(self.buffer, target, self.semaphores.at[at])
            copy.start()
            self.copies.append(copy)

    def finish(self):
        for copy in self.copies:
            copy.wait()


def whole(scalars, ref, buffer):
    return [(ref, buffer)]


def columns_of(layer):
    def view(scalars, ref, buffer):
        pairs = [pl.ds(2 * at, 2) for at in range(KVH // 2)]
        return [(ref.at[pair, layer], buffer.at[pair]) for pair in pairs]

    return view


def call(kernel, name, results, scalars, operands):
    arrays = [o[0] if isinstance(o, tuple) else o for o in operands]
    manual_in = [isinstance(o, tuple) for o in operands]
    manual_out = [len(r) == 3 for r in results]
    n_scalars, n_arrays, n_results = len(scalars), len(arrays), len(results)
    most = KVH // 2

    def body(*refs):
        scalar_refs = refs[:n_scalars]
        ins = list(refs[n_scalars : n_scalars + n_arrays])
        outs = list(refs[n_scalars + n_arrays : n_scalars + n_arrays + n_results])
        scratch = list(refs[n_scalars + n_arrays + n_results :])
        in_semaphores, out_semaphores = scratch.pop(), None
        out_semaphores, in_semaphores = in_semaphores, scratch.pop()
        loads, stores = [], []
        for at in range(n_arrays):
            if manual_in[at]:
                buffer = scratch.pop(0)
                pairs = operands[at][2](scalar_refs, ins[at], buffer)
                copies = [
                    pltpu.make_async_copy(*pair, in_semaphores.at[at * most + k])
                    for k, pair in enumerate(pairs)
                ]
                ins[at] = Loaded(buffer, copies)
                loads.append(ins[at])
        for at in range(n_results):
            if manual_out[at]:
                outs[at] = Stored(scratch.pop(0), outs[at], out_semaphores.at[at])
                stores.append(outs[at])
        kernel(*scalar_refs, *ins, *outs)
        for load in loads:
            load()
        for store in stores:
            store.finish()

    moved = sum(a.size * a.dtype.itemsize for a in arrays)
    moved += sum(math.prod(r[0]) * jnp.dtype(r[1]).itemsize for r in results)
    in_vmem = pl.BlockSpec(memory_space=pltpu.VMEM)
    in_hbm = pl.BlockSpec(memory_space=pltpu.HBM)
    return pl.pallas_call(
        body,
        out_shape=[jax.ShapeDtypeStruct(r[0], r[1]) for r in results],
        in_specs=[pl.BlockSpec(memory_space=pltpu.SMEM)] * n_scalars
        + [in_hbm if manual else in_vmem for manual in manual_in],
        out_specs=[in_hbm if manual else in_vmem for manual in manual_out],
        scratch_shapes=[pltpu.VMEM(o[1], o[0].dtype) for o in operands if isinstance(o, tuple)]
        + [pltpu.VMEM(r[2], r[1]) for r in results if len(r) == 3]
        + [
            pltpu.SemaphoreType.DMA((n_arrays * most,)),
            pltpu.SemaphoreType.DMA((n_results, PEERS)),
        ],
        compiler_params=pltpu.CompilerParams(vmem_limit_bytes=VMEM_BYTES),
        cost_estimate=pl.CostEstimate(flops=0, bytes_accessed=moved, transcendentals=0),
        name=name,
    )(*scalars, *arrays)


def pack_kernel(core, visual, queries, keys, down, up, gain, out):
    other = 1 - core[0]
    at = pl.multiple_of(other * HALF, HALF)
    key_at = pl.multiple_of(other * HD, HD)
    out[R_VIS:R_Q, :] = visual[:, pl.ds(at, HALF)]
    out[R_Q:R_K, :] = queries[:, pl.ds(at, HALF)]
    for j in range(8):
        out[R_K:R_DN, j * HD : (j + 1) * HD] = keys[j * 32 : (j + 1) * 32, pl.ds(key_at, HD)]
    out[R_DN:R_UP, :] = down[:, pl.ds(at, HALF)]
    out[R_UP:R_GN, :] = up[...]
    out[R_GN:R_END, :] = gain[:, pl.ds(at, HALF)]


def softmax_of(query_rows, key_rows, length):
    scores = nt(stack_heads(query_rows), key_rows) / math.sqrt(HD)
    shape = scores.shape
    row = lax.rem(lax.broadcasted_iota(jnp.int32, shape, 0), SEQ)
    column = lax.broadcasted_iota(jnp.int32, shape, 1)
    allowed = (column <= row) & (column < length)
    scores = jnp.where(allowed, scores, -jnp.inf)
    top = jnp.max(scores, axis=-1, keepdims=True)
    weights = jnp.exp(scores - top)
    return (weights / jnp.sum(weights, axis=-1, keepdims=True)).astype(BF)


def prepare_kernel(
    core, counts, starts, lengths,
    received, visual, queries, keys, down, up, gain, embeddings, cotangent,
    weights, entry, cotangent_half, downs, ups, gains, payload,
):
    own = core[0]
    other = 1 - own
    half = pl.ds(pl.multiple_of(own * HALF, HALF), HALF)
    key_half = pl.ds(pl.multiple_of(own * HD, HD), HD)
    downs[own] = down[:, half]
    downs[other] = received[R_DN:R_UP, :]
    ups[own] = up[...]
    ups[other] = received[R_UP:R_GN, :]
    gains[own] = gain[:, half]
    gains[other] = received[R_GN:R_END, :]
    position = lax.broadcasted_iota(jnp.int32, (SEQ, VIS), 0)
    slot = lax.broadcasted_iota(jnp.int32, (SEQ, VIS), 1)
    place = lax.broadcasted_iota(jnp.int32, (SEQ, 1), 0)
    for index, table in ((own, visual[:, half]), (other, received[R_VIS:R_Q, :])):
        begin = starts[index]
        count = counts[index] * TOKT
        placing = ((position == begin + slot) & (slot < count)).astype(F32).astype(BF)
        inserted = nn(placing, table).astype(BF)
        covered = (place >= begin) & (place < begin + count)
        rows = pl.ds(pl.multiple_of(index * SEQ, SEQ), SEQ)
        entry[rows, :] = jnp.where(covered, inserted, embeddings[index, :, half])
    for m in range(MB):
        rows = slice(m * SEQ, (m + 1) * SEQ)
        cotangent_half[rows, :] = cotangent[m, :, half]
        weights[own, m] = softmax_of(queries[rows, half], keys[rows, key_half], lengths[m])
        other_keys = jnp.concatenate(
            [received[R_K:R_DN, j * HD : (j + 1) * HD] for j in range(4 * m, 4 * m + 4)], axis=0
        )
        weights[other, m] = softmax_of(
            received[R_Q + m * SEQ : R_Q + (m + 1) * SEQ, :], other_keys, lengths[m]
        )
    value_gradient = jnp.concatenate(
        [
            tn(weights[1, m], stack_heads(cotangent_half[m * SEQ : (m + 1) * SEQ, :]))
            for m in range(MB)
        ],
        axis=0,
    ).astype(BF)
    entry_float = entry[...].astype(F32)
    squares = jnp.sum(entry_float * entry_float, axis=-1, keepdims=True)
    gained = (entry_float * gains[0][0:1, :].astype(F32)).astype(BF)
    block = payload_block(value_gradient, squares, nt(downs[0], gained))
    for peer in range(PEERS):
        payload[peer] = block


def entry_norm_kernel(
    core, received, entry, ups, gains,
    normed, sums, adapter_rows, full_gradient, own_gradient, lora_gradient,
):
    rows, low_rank = total_of_payloads(received)
    sums[...] = rows
    column = inverse_of(rows_to_columns(rows)[:, 0:1])
    adapter_rows[...] = low_rank * inverse_of(rows[0:1, :])
    gain = gains[0][0:1, :].astype(F32)
    normed[...] = (entry[...].astype(F32) * column * gain).astype(BF)
    for head in range(KVH):
        full_gradient[:, head * HD : (head + 1) * HD] = received[block_of(head), :ROWS, :]
    own_gradient[...] = received[core[0] * 4 + core[1], :ROWS, :]
    lora_gradient[...] = ADAPTER_SCALE * nt(ups[1], full_gradient[...])


def partial_values(rows, down, up, columns, out):
    adapter = (ADAPTER_SCALE * nt(rows, down)).astype(BF)
    for pair in range(KVH // 2):
        weight = columns(pair)[2 * pair : 2 * pair + 2].reshape(2 * HD, HALF)
        span = slice(2 * pair * HD, (2 * pair + 2) * HD)
        partial = (nt(rows, weight) + nn(adapter, up[:, span])).astype(BF)
        for at in range(2):
            out[block_of(2 * pair + at)] = partial[:, at * HD : (at + 1) * HD]


def first_values_kernel(normed, downs, ups, columns, out):
    partial_values(normed[...], downs[0], ups[0], columns, out)


def second_values_kernel(hidden, totals, gains, downs, ups, columns, out):
    column = inverse_of(rows_to_columns(totals[...])[:, 0:1])
    gain = gains[1][0:1, :].astype(F32)
    normed = (hidden[...].astype(F32) * gain * column).astype(BF)
    partial_values(normed, downs[1], ups[1], columns, out)


def weighted_gradient(gradient_of, lora_gradient, down, gain, columns):
    grad = tn(lora_gradient.astype(BF), down)
    for pair in range(KVH // 2):
        weight = columns(pair)[2 * pair : 2 * pair + 2].reshape(2 * HD, HALF)
        grad = grad + nn(gradient_of(pair), weight)
    return grad * gain[0:1, :].astype(F32)


def scaled_kernel(full_gradient, lora_gradient, downs, gains, columns, scaled):
    scaled[...] = weighted_gradient(
        lambda pair: full_gradient[:, 2 * pair * HD : (2 * pair + 2) * HD],
        lora_gradient[...],
        downs[1],
        gains[1],
        columns,
    )


def attended_rows(weights, layer, value_rows):
    return jnp.concatenate(
        [
            unstack_heads(nn(weights[layer, m], value_rows[m * SEQ : (m + 1) * SEQ, :]))
            for m in range(MB)
        ],
        axis=0,
    )


def first_output_kernel(received, weights, entry, scaled, hidden, value_rows, payload):
    values = received[0].astype(F32)
    for peer in range(1, PEERS):
        values = values + received[peer].astype(F32)
    value_rows[...] = values
    attended = attended_rows(weights, 0, values.astype(BF))
    output = (entry[...].astype(F32) + attended).astype(BF)
    hidden[...] = output
    output_float = output.astype(F32)
    squares = jnp.sum(output_float * output_float, axis=-1, keepdims=True)
    dots = jnp.sum(output_float * scaled[...], axis=-1, keepdims=True)
    block = columns_to_rows(squares, dots)
    for peer in range(PEERS):
        payload[peer] = block


def first_gradient_kernel(
    received, hidden, scaled, cotangent_half, weights, value_rows, gains, downs, lora_gradient,
    gradient, totals, down_gradient, payload,
):
    total = received[0]
    for peer in range(1, PEERS):
        total = total + received[peer]
    totals[...] = total
    sums = rows_to_columns(total)
    column = inverse_of(sums[:, 0:1])
    factor = column * column * column * sums[:, 1:2] / MODEL_WIDTH
    hidden_float = hidden[...].astype(F32)
    grad = (
        cotangent_half[...].astype(F32) + column * scaled[...] - hidden_float * factor
    ).astype(BF)
    gradient.buffer[...] = grad
    gradient.send()
    gained = hidden_float * gains[1][0:1, :].astype(F32)
    low_rank = nt(downs[1], gained.astype(BF))
    value_gradient = jnp.concatenate(
        [tn(weights[0, m], stack_heads(grad[m * SEQ : (m + 1) * SEQ, :])) for m in range(MB)],
        axis=0,
    ).astype(BF)
    dots = jnp.sum(value_gradient.astype(F32) * value_rows[...], axis=-1, keepdims=True)
    payload.buffer[...] = payload_block(value_gradient, dots, low_rank)
    payload.send(repeated=True)
    normed = (gained * column).astype(BF)
    down_gradient[...] = nn(lora_gradient[...].astype(BF), normed)


def gathered_gradient(received):
    return jnp.concatenate([received[block_of(head), :ROWS, :] for head in range(KVH)], axis=1)


def map_gradient_kernel(
    core, received, ups, adapter_0, totals, gradient_1, down_gradient_1, normed_0, out
):
    rows, low_rank = total_of_payloads(received)
    lora_0 = ADAPTER_SCALE * nt(ups[0], gathered_gradient(received))
    own = received[core[0] * 4 + core[1], :ROWS, :]
    adapter_1 = (low_rank * inverse_of(totals[0:1, :])).astype(BF)
    down = (nn(lora_0.astype(BF), normed_0()[...]), down_gradient_1[...])
    up = (
        ADAPTER_SCALE * nn(adapter_0[...].astype(BF), own),
        ADAPTER_SCALE * nn(adapter_1, gradient_1[...]),
    )
    for layer in range(2):
        for y in range(8):
            block = out.at[layer * 8 + y]
            block[:RANK, :] = down[layer][:, y * HD : (y + 1) * HD]
            block[RANK : RANK + 2, :] = up[layer][2 * y : 2 * y + 2, :]
            block[RANK + 2 :, :] = jnp.zeros((M_ROWS - RANK - 2, HD), F32)


def near_sum_kernel(received, out):
    for half in range(2):
        total = received[half * 8]
        for y in range(1, 8):
            total = total + received[half * 8 + y]
        for peer in range(KVH):
            out[peer, half] = total.astype(BF)


def far_sum_kernel(received, out):
    total = received[0].astype(F32)
    for z in range(1, KVH):
        total = total + received[z].astype(F32)
    for peer in range(8):
        out[peer] = total.astype(BF)


def maps_kernel(received, down_sum, up_sum, *, scale):
    for half in range(2):
        for y in range(8):
            block = received[y, half].astype(F32) * scale
            at = half * HALF + y * HD
            down_sum[:, at : at + HD] = block[:RANK, :]
            up_sum[2 * y : 2 * y + 2, half * HD : (half + 1) * HD] = block[RANK : RANK + 2, :]


def slot_gradient_kernel(
    counts, starts, received, ups, downs, gains, sums, columns, gradient, entry, slots
):
    rows, _ = total_of_payloads(received)
    lora_gradient = ADAPTER_SCALE * nt(ups[0], gathered_gradient(received))
    scaled = weighted_gradient(
        lambda pair: jnp.concatenate(
            [received[block_of(2 * pair + at), :ROWS, :] for at in range(2)], axis=1
        ),
        lora_gradient,
        downs[0],
        gains[0],
        columns,
    )
    column = inverse_of(rows_to_columns(sums[...])[:, 0:1])
    factor = column * column * rows_to_columns(rows)[:, 0:1] / MODEL_WIDTH
    grad = (
        gradient()[...].astype(F32) + column * scaled - entry()[...].astype(F32) * factor
    ).astype(BF)
    slot = lax.broadcasted_iota(jnp.int32, (VIS, SEQ), 0)
    position = lax.broadcasted_iota(jnp.int32, (VIS, SEQ), 1)
    for m in range(MB):
        picking = ((position == starts[m] + slot) & (slot < counts[m] * TOKT)).astype(F32).astype(BF)
        slots[m] = nn(picking, grad[m * SEQ : (m + 1) * SEQ, :]).astype(BF)


def second_output_kernel(values, weights, hidden, out):
    attended = attended_rows(weights, 1, values[...])
    out[...] = (hidden[...].astype(F32) + attended).astype(BF)


def swap_cores(block):
    return lax.ppermute(block, "section", [(0, 1), (1, 0)])


def to_heads(block):
    return lax.all_to_all(block, ("section", "tp"), 0, 0)


def on_device(
    embeddings,
    visual,
    image_block_count,
    starts,
    lengths,
    queries,
    layer_key_vectors,
    input_norm_gain,
    frozen_value_weight,
    adapter_down_map,
    adapter_up_map,
    cotangent,
):
    section = lax.axis_index("section")
    tp = lax.axis_index("tp")
    n_fsdp = lax.axis_size("fsdp")
    n_y = n_fsdp // KVH
    core = jnp.stack([section, tp]).astype(jnp.int32)
    counts = image_block_count[:, 0]
    begins = starts[:, 0]
    seq_lengths = lengths[:, 0]

    shard = frozen_value_weight[0].T
    pieces = shard.reshape(shard.shape[0], 2, HALF).transpose(1, 0, 2)
    pieces = jnp.broadcast_to(pieces[:, None], (2, n_y) + pieces.shape[1:])
    pieces = pieces.reshape((2 * n_y,) + pieces.shape[2:])
    head_groups = [
        [s * n_fsdp + z * n_y + y for s in range(2) for y in range(n_y)] for z in range(KVH)
    ]
    head_columns = lax.all_to_all(
        pieces, ("section", "fsdp"), 0, 0, axis_index_groups=head_groups
    ).reshape(2, HD, HALF)
    row_groups = [[z * n_y + y for z in range(KVH)] for y in range(n_y)]
    columns = lax.all_gather(head_columns, "fsdp", axis=0, axis_index_groups=row_groups)

    own = (
        visual[0, 0],
        queries[0].reshape(ROWS, 2 * HALF),
        layer_key_vectors[0].reshape(ROWS, 2 * HD),
        adapter_down_map[0].T,
        adapter_up_map[0],
        jnp.broadcast_to(input_norm_gain, (RANK, 2 * HALF)),
    )
    (packed,) = call(pack_kernel, "pack", [((R_END, HALF), BF)], (core,), own)

    wide = ((ROWS, HALF), BF)
    low = ((RANK, ROWS), F32)
    sums = ((SUBLANES, ROWS), F32)
    maps = ((2, RANK, HALF), BF)
    blocks = ((PEERS, ROWS, HD), BF)
    mixed = ((PEERS, R_PAY, HD), BF)
    weights, entry, cotangent_half, downs, ups, gains, payload = call(
        prepare_kernel,
        "prepare",
        [((2, MB, HEADS * SEQ, SEQ), BF), wide, wide, maps, maps, maps, mixed],
        (core, counts, begins, seq_lengths),
        (swap_cores(packed), *own, embeddings, cotangent),
    )

    def weight_of(layer):
        return (columns, (KVH, HD, HALF), columns_of(layer))

    normed_0, sums_0, adapter_0, full_gradient_1, own_gradient_1, lora_gradient_1 = call(
        entry_norm_kernel,
        "entry_norm",
        [wide, sums, low, wide, ((ROWS, HD), BF), low],
        (core,),
        (to_heads(payload), entry, ups, gains),
    )
    (partial_0,) = call(
        first_values_kernel, "values_0", [blocks], (), (normed_0, downs, ups, weight_of(0))
    )
    (scaled_1,) = call(
        scaled_kernel,
        "scaled_1",
        [((ROWS, HALF), F32)],
        (),
        (full_gradient_1, lora_gradient_1, downs, gains, weight_of(1)),
    )
    hidden_0, value_rows, payload = call(
        first_output_kernel,
        "first_output",
        [wide, ((ROWS, HD), F32), ((PEERS, SUBLANES, ROWS), F32)],
        (),
        (to_heads(partial_0), weights, entry, scaled_1),
    )
    gradient, totals, down_gradient_1, payload = call(
        first_gradient_kernel,
        "first_gradient",
        [
            wide + ((ROWS, HALF),),
            sums,
            ((RANK, HALF), F32),
            mixed + ((R_PAY, HD),),
        ],
        (),
        (
            to_heads(payload),
            hidden_0,
            scaled_1,
            cotangent_half,
            weights,
            value_rows,
            gains,
            downs,
            lora_gradient_1,
        ),
    )
    gathered = to_heads(payload)
    (partial_1,) = call(
        second_values_kernel,
        "values_1",
        [blocks],
        (),
        (hidden_0, totals, gains, downs, ups, weight_of(1)),
    )
    values_1 = lax.psum_scatter(partial_1, ("section", "tp"), scatter_dimension=0)

    (chunks,) = call(
        map_gradient_kernel,
        "map_gradient",
        [((2 * n_y, M_ROWS, HD), F32)],
        (core,),
        (
            gathered,
            ups,
            adapter_0,
            totals,
            own_gradient_1,
            down_gradient_1,
            (normed_0, normed_0.shape, whole),
        ),
    )
    halves_of_maps = ((8, 2, M_ROWS, HD), BF)
    near = lax.all_to_all(chunks, ("section", "fsdp"), 0, 0, axis_index_groups=head_groups)
    (near,) = call(near_sum_kernel, "near_sum", [halves_of_maps], (), (near,))
    far = lax.all_to_all(near, "fsdp", 0, 0, axis_index_groups=row_groups)
    (far,) = call(far_sum_kernel, "far_sum", [halves_of_maps], (), (far,))
    y_groups = [[z * n_y + y for y in range(n_y)] for z in range(KVH)]
    summed = lax.all_to_all(far, "fsdp", 0, 0, axis_index_groups=y_groups)
    down_sum, up_sum = call(
        functools.partial(maps_kernel, scale=1.0 / math.sqrt(MB * SEQ * n_fsdp)),
        "maps",
        [((RANK, 2 * HALF), F32), ((RANK, 2 * HD), F32)],
        (),
        (summed,),
    )

    (slots,) = call(
        slot_gradient_kernel,
        "slot_gradient",
        [((MB, VIS, HALF), BF)],
        (counts, begins),
        (
            gathered,
            ups,
            downs,
            gains,
            sums_0,
            weight_of(0),
            (gradient, gradient.shape, whole),
            (entry, entry.shape, whole),
        ),
    )
    (hidden_1,) = call(
        second_output_kernel, "second_output", [wide], (), (values_1, weights, hidden_0)
    )

    first = section == 0

    def halves(mine, theirs):
        left = jnp.where(first, mine, theirs)
        right = jnp.where(first, theirs, mine)
        return jnp.concatenate([left, right], axis=-1)

    slot_rows = halves(
        jnp.where(first, slots[0], slots[1]), swap_cores(jnp.where(first, slots[1], slots[0]))
    )
    hidden = halves(
        jnp.where(first, hidden_0, hidden_1), swap_cores(jnp.where(first, hidden_1, hidden_0))
    )
    return (
        hidden.reshape(1, MB, SEQ, 2 * HALF),
        slot_rows[None, None],
        down_sum.T[None],
        up_sum[None],
    )


def solution(mesh):
    return jax.shard_map(
        on_device,
        mesh=mesh,
        in_specs=(
            P(None, "fsdp", "tp"),
            P("section", "fsdp", None, "tp"),
            P(None, "fsdp"),
            P(None, "fsdp"),
            P(None, "fsdp"),
            P("section", None, "fsdp", "tp"),
            P("section", None, "fsdp", "tp"),
            P("section", "tp"),
            P("section", "tp", "fsdp"),
            P("section", "tp", None),
            P("section", None, None),
            P(None, "fsdp", "tp"),
        ),
        out_specs=(
            P("section", None, "fsdp", "tp"),
            P("section", "fsdp", None, "tp"),
            P("section", "tp", None),
            P("section", None, "tp"),
        ),
        check_vma=False,
    )
```

```python
import functools
import math

import jax
import jax.numpy as jnp
from jax import lax
from jax.experimental import pallas as pl
from jax.experimental.pallas import tpu as pltpu
from jax.sharding import PartitionSpec as P

MODEL_WIDTH = 8192
HD = 128
TOKT = 32
ADAPTER_SCALE = 0.5
EPS = 1e-06

SEQ = 128
MB = 2
ROWS = MB * SEQ
VIS = 96
RANK = 16
HEADS = 8
HALF = HEADS * HD
KVH = 8
PEERS = 8
VMEM_BYTES = 40 * 1024 * 1024

BF = jnp.bfloat16
F32 = jnp.float32

R_VIS, R_Q, R_K, R_DN, R_UP, R_GN, R_END = 0, 96, 352, 384, 400, 416, 432
R_SUM, R_LOW, R_PAY = ROWS, ROWS + RANK, ROWS + RANK + 2 * RANK
SUBLANES = 8
M_ROWS = RANK + SUBLANES


def block_of(head):
    return (head % 2) * 4 + head // 2


def nt(left, right):
    return lax.dot_general(left, right, (((1,), (1,)), ((), ())), preferred_element_type=F32)


def tn(left, right):
    return lax.dot_general(left, right, (((0,), (0,)), ((), ())), preferred_element_type=F32)


def nn(left, right):
    return jnp.dot(left, right, preferred_element_type=F32)


def stack_heads(block):
    return jnp.concatenate([block[:, h * HD : (h + 1) * HD] for h in range(HEADS)], axis=0)


def unstack_heads(block):
    return jnp.concatenate([block[h * SEQ : (h + 1) * SEQ, :] for h in range(HEADS)], axis=1)


def columns_to_rows(*columns):
    lane = lax.broadcasted_iota(jnp.int32, (ROWS, HD), 1)
    square = jnp.zeros((ROWS, HD), F32)
    for at, column in enumerate(columns):
        square = jnp.where(lane == at, column, square)
    return square.T[:SUBLANES, :]


def rows_to_columns(rows):
    padded = jnp.concatenate([rows, jnp.zeros((HD - SUBLANES, ROWS), F32)], axis=0)
    return padded.T


def payload_block(values, column, low_rank):
    row = columns_to_rows(column)[0:1, :]
    high = row.astype(BF).astype(F32)
    low = row - high
    at = lax.broadcasted_iota(jnp.int32, (RANK, HD), 0)
    sums = jnp.zeros((RANK, HD), F32)
    for index, part in enumerate((high[:, :HD], high[:, HD:], low[:, :HD], low[:, HD:])):
        sums = jnp.where(at == index, part, sums)
    low_rank = low_rank.astype(BF)
    return jnp.concatenate(
        [values, sums.astype(BF), low_rank[:, :HD], low_rank[:, HD:]], axis=0
    )


def total_of_payloads(blocks):
    sums = blocks[0, R_SUM:R_LOW, :].astype(F32)
    low_rank = blocks[0, R_LOW:, :].astype(F32)
    for peer in range(1, PEERS):
        sums = sums + blocks[peer, R_SUM:R_LOW, :].astype(F32)
        low_rank = low_rank + blocks[peer, R_LOW:, :].astype(F32)
    left = sums[0:1, :] + sums[2:3, :]
    right = sums[1:2, :] + sums[3:4, :]
    row = jnp.concatenate([left, right], axis=1)
    at = lax.broadcasted_iota(jnp.int32, (SUBLANES, ROWS), 0)
    rows = jnp.where(at == 0, row, 0.0)
    return rows, jnp.concatenate([low_rank[:RANK, :], low_rank[RANK:, :]], axis=1)


def inverse_of(squares):
    return lax.rsqrt(squares / MODEL_WIDTH + EPS)


def call(kernel, name, results, scalars, arrays, after=(), scratch=()):
    n_read = len(scalars) + len(arrays)

    def body(*refs):
        kernel(*refs[:n_read], *refs[n_read + len(after) :])

    moved = sum(a.size * a.dtype.itemsize for a in arrays)
    moved += sum(math.prod(shape) * jnp.dtype(dtype).itemsize for shape, dtype in results)
    in_vmem = pl.BlockSpec(memory_space=pltpu.VMEM)
    anywhere = pl.BlockSpec(memory_space=pl.ANY)
    return pl.pallas_call(
        body,
        out_shape=[jax.ShapeDtypeStruct(shape, dtype) for shape, dtype in results],
        in_specs=[pl.BlockSpec(memory_space=pltpu.SMEM)] * len(scalars)
        + [in_vmem] * len(arrays)
        + [anywhere] * len(after),
        out_specs=[in_vmem] * len(results),
        scratch_shapes=list(scratch),
        compiler_params=pltpu.CompilerParams(vmem_limit_bytes=VMEM_BYTES),
        cost_estimate=pl.CostEstimate(flops=0, bytes_accessed=moved, transcendentals=0),
        name=name,
    )(*scalars, *arrays, *after)


def pack_kernel(core, visual, queries, keys, down, up, gain, out):
    other = 1 - core[0]
    at = pl.multiple_of(other * HALF, HALF)
    key_at = pl.multiple_of(other * HD, HD)
    out[R_VIS:R_Q, :] = visual[:, pl.ds(at, HALF)]
    out[R_Q:R_K, :] = queries[:, pl.ds(at, HALF)]
    for j in range(8):
        out[R_K:R_DN, j * HD : (j + 1) * HD] = keys[j * 32 : (j + 1) * 32, pl.ds(key_at, HD)]
    out[R_DN:R_UP, :] = down[:, pl.ds(at, HALF)]
    out[R_UP:R_GN, :] = up[...]
    out[R_GN:R_END, :] = gain[:, pl.ds(at, HALF)]


def softmax_of(query_rows, key_rows, length):
    scores = nt(stack_heads(query_rows), key_rows) / math.sqrt(HD)
    shape = scores.shape
    row = lax.rem(lax.broadcasted_iota(jnp.int32, shape, 0), SEQ)
    column = lax.broadcasted_iota(jnp.int32, shape, 1)
    allowed = (column <= row) & (column < length)
    scores = jnp.where(allowed, scores, -jnp.inf)
    top = jnp.max(scores, axis=-1, keepdims=True)
    weights = jnp.exp(scores - top)
    return (weights / jnp.sum(weights, axis=-1, keepdims=True)).astype(BF)


def prepare_kernel(
    core, counts, starts, lengths,
    received, visual, queries, keys, down, up, gain, embeddings, cotangent,
    weights, entry, cotangent_half, downs, ups, gains, payload,
):
    own = core[0]
    other = 1 - own
    half = pl.ds(pl.multiple_of(own * HALF, HALF), HALF)
    key_half = pl.ds(pl.multiple_of(own * HD, HD), HD)
    downs[own] = down[:, half]
    downs[other] = received[R_DN:R_UP, :]
    ups[own] = up[...]
    ups[other] = received[R_UP:R_GN, :]
    gains[own] = gain[:, half]
    gains[other] = received[R_GN:R_END, :]
    position = lax.broadcasted_iota(jnp.int32, (SEQ, VIS), 0)
    slot = lax.broadcasted_iota(jnp.int32, (SEQ, VIS), 1)
    place = lax.broadcasted_iota(jnp.int32, (SEQ, 1), 0)
    for index, table in ((own, visual[:, half]), (other, received[R_VIS:R_Q, :])):
        begin = starts[index]
        count = counts[index] * TOKT
        placing = ((position == begin + slot) & (slot < count)).astype(F32).astype(BF)
        inserted = nn(placing, table).astype(BF)
        covered = (place >= begin) & (place < begin + count)
        rows = pl.ds(pl.multiple_of(index * SEQ, SEQ), SEQ)
        entry[rows, :] = jnp.where(covered, inserted, embeddings[index, :, half])
    for m in range(MB):
        rows = slice(m * SEQ, (m + 1) * SEQ)
        cotangent_half[rows, :] = cotangent[m, :, half]
        weights[own, m] = softmax_of(queries[rows, half], keys[rows, key_half], lengths[m])
        other_keys = jnp.concatenate(
            [received[R_K:R_DN, j * HD : (j + 1) * HD] for j in range(4 * m, 4 * m + 4)], axis=0
        )
        weights[other, m] = softmax_of(
            received[R_Q + m * SEQ : R_Q + (m + 1) * SEQ, :], other_keys, lengths[m]
        )
    value_gradient = jnp.concatenate(
        [
            tn(weights[1, m], stack_heads(cotangent_half[m * SEQ : (m + 1) * SEQ, :]))
            for m in range(MB)
        ],
        axis=0,
    ).astype(BF)
    entry_float = entry[...].astype(F32)
    squares = jnp.sum(entry_float * entry_float, axis=-1, keepdims=True)
    gained = (entry_float * gains[0][0:1, :].astype(F32)).astype(BF)
    block = payload_block(value_gradient, squares, nt(downs[0], gained))
    for peer in range(PEERS):
        payload[peer] = block


def entry_norm_kernel(
    core, received, entry, ups, gains,
    normed, sums, adapter_rows, full_gradient, own_gradient, lora_gradient,
):
    rows, low_rank = total_of_payloads(received)
    sums[...] = rows
    column = inverse_of(rows_to_columns(rows)[:, 0:1])
    adapter_rows[...] = low_rank * inverse_of(rows[0:1, :])
    gain = gains[0][0:1, :].astype(F32)
    normed[...] = (entry[...].astype(F32) * column * gain).astype(BF)
    for head in range(KVH):
        full_gradient[:, head * HD : (head + 1) * HD] = received[block_of(head), :ROWS, :]
    own_gradient[...] = received[core[0] * 4 + core[1], :ROWS, :]
    lora_gradient[...] = ADAPTER_SCALE * nt(ups[1], full_gradient[...])


def partial_values(rows, down, up, columns, out):
    adapter = (ADAPTER_SCALE * nt(rows, down)).astype(BF)
    for pair in range(KVH // 2):
        weight = columns[2 * pair : 2 * pair + 2].reshape(2 * HD, HALF)
        span = slice(2 * pair * HD, (2 * pair + 2) * HD)
        partial = (nt(rows, weight) + nn(adapter, up[:, span])).astype(BF)
        for at in range(2):
            out[block_of(2 * pair + at)] = partial[:, at * HD : (at + 1) * HD]


def first_values_kernel(normed, downs, ups, columns, out):
    partial_values(normed[...], downs[0], ups[0], columns, out)


def weighted_gradient(gradient_of, lora_gradient, down, gain, columns):
    grad = tn(lora_gradient.astype(BF), down)
    for pair in range(KVH // 2):
        weight = columns[2 * pair : 2 * pair + 2].reshape(2 * HD, HALF)
        grad = grad + nn(gradient_of(pair), weight)
    return grad * gain[0:1, :].astype(F32)


def scaled_kernel(full_gradient, lora_gradient, downs, gains, columns, scaled):
    grad = weighted_gradient(
        lambda pair: full_gradient[:, 2 * pair * HD : (2 * pair + 2) * HD],
        lora_gradient[...],
        downs[1],
        gains[1],
        columns,
    )
    scaled[...] = grad.astype(BF)


def attended_rows(weights, layer, value_rows):
    return jnp.concatenate(
        [
            unstack_heads(nn(weights[layer, m], value_rows[m * SEQ : (m + 1) * SEQ, :]))
            for m in range(MB)
        ],
        axis=0,
    )


def first_output_kernel(
    received, weights, entry, scaled, gains, downs, ups, columns,
    hidden, value_rows, payload, partial,
):
    values = received[0].astype(F32)
    for peer in range(1, PEERS):
        values = values + received[peer].astype(F32)
    value_rows[...] = values
    attended = attended_rows(weights, 0, values.astype(BF))
    output = (entry[...].astype(F32) + attended).astype(BF)
    hidden[...] = output
    output_float = output.astype(F32)
    squares = jnp.sum(output_float * output_float, axis=-1, keepdims=True)
    dots = jnp.sum(output_float * scaled[...].astype(F32), axis=-1, keepdims=True)
    block = columns_to_rows(squares, dots)
    for peer in range(PEERS):
        payload[peer] = block
    gained = (output_float * gains[1][0:1, :].astype(F32)).astype(BF)
    partial_values(gained, downs[1], ups[1], columns, partial)


def first_gradient_kernel(
    received, hidden, scaled, cotangent_half, weights, value_rows, gains, downs, lora_gradient,
    gradient, totals, down_gradient, payload,
):
    total = received[0]
    for peer in range(1, PEERS):
        total = total + received[peer]
    totals[...] = total
    sums = rows_to_columns(total)
    column = inverse_of(sums[:, 0:1])
    factor = column * column * column * sums[:, 1:2] / MODEL_WIDTH
    hidden_float = hidden[...].astype(F32)
    grad = (
        cotangent_half[...].astype(F32) + column * scaled[...].astype(F32) - hidden_float * factor
    ).astype(BF)
    gradient[...] = grad
    gained = hidden_float * gains[1][0:1, :].astype(F32)
    low_rank = nt(downs[1], gained.astype(BF))
    value_gradient = jnp.concatenate(
        [tn(weights[0, m], stack_heads(grad[m * SEQ : (m + 1) * SEQ, :])) for m in range(MB)],
        axis=0,
    ).astype(BF)
    dots = jnp.sum(value_gradient.astype(F32) * value_rows[...], axis=-1, keepdims=True)
    block = payload_block(value_gradient, dots, low_rank)
    for peer in range(PEERS):
        payload[peer] = block
    normed = (gained * column).astype(BF)
    down_gradient[...] = nn(lora_gradient[...].astype(BF), normed)


def gathered_gradient(received):
    return jnp.concatenate([received[block_of(head), :ROWS, :] for head in range(KVH)], axis=1)


def map_gradient_kernel(
    core, received, ups, adapter_0, totals, gradient_1, down_gradient_1, normed_0, out
):
    rows, low_rank = total_of_payloads(received)
    lora_0 = ADAPTER_SCALE * nt(ups[0], gathered_gradient(received))
    own = received[core[0] * 4 + core[1], :ROWS, :]
    adapter_1 = (low_rank * inverse_of(totals[0:1, :])).astype(BF)
    down = (nn(lora_0.astype(BF), normed_0[...]), down_gradient_1[...])
    up = (
        ADAPTER_SCALE * nn(adapter_0[...].astype(BF), own),
        ADAPTER_SCALE * nn(adapter_1, gradient_1[...]),
    )
    for layer in range(2):
        for y in range(8):
            block = out.at[layer * 8 + y]
            block[:RANK, :] = down[layer][:, y * HD : (y + 1) * HD]
            block[RANK : RANK + 2, :] = up[layer][2 * y : 2 * y + 2, :]
            block[RANK + 2 :, :] = jnp.zeros((M_ROWS - RANK - 2, HD), F32)


def near_sum_kernel(received, out):
    for half in range(2):
        total = received[half * 8]
        for y in range(1, 8):
            total = total + received[half * 8 + y]
        for peer in range(KVH):
            out[peer, half] = total.astype(BF)


def far_sum_kernel(received, out):
    total = received[0].astype(F32)
    for z in range(1, KVH):
        total = total + received[z].astype(F32)
    for peer in range(8):
        out[peer] = total.astype(BF)


def finish_kernel(
    core, received, own_hidden, other_hidden, own_slots, other_slots,
    hidden, slots, down_sum, up_sum, semaphores, *, scale,
):
    copies = []
    own = core[0]
    for at, (part, own_part, other_part) in enumerate(
        ((hidden, own_hidden, other_hidden), (slots, own_slots, other_slots))
    ):
        for k, (half, block) in enumerate(((own, own_part), (1 - own, other_part))):
            to = pl.ds(pl.multiple_of(half * HALF, HALF), HALF)
            copy = pltpu.make_async_copy(block, part.at[:, to], semaphores.at[2 * at + k])
            copy.start()
            copies.append(copy)
    for half in range(2):
        for y in range(8):
            block = received[y, half].astype(F32) * scale
            at = half * HALF + y * HD
            down_sum[:, at : at + HD] = block[:RANK, :]
            up_sum[2 * y : 2 * y + 2, half * HD : (half + 1) * HD] = block[RANK : RANK + 2, :]
    for copy in copies:
        copy.wait()


def slot_gradient_kernel(
    core, counts, starts,
    received, ups, downs, gains, sums, columns, gradient, entry,
    own_slots, other_slots,
):
    rows, _ = total_of_payloads(received)
    lora_gradient = ADAPTER_SCALE * nt(ups[0], gathered_gradient(received))
    scaled = weighted_gradient(
        lambda pair: jnp.concatenate(
            [received[block_of(2 * pair + at), :ROWS, :] for at in range(2)], axis=1
        ),
        lora_gradient,
        downs[0],
        gains[0],
        columns,
    )
    column = inverse_of(rows_to_columns(sums[...])[:, 0:1])
    factor = column * column * rows_to_columns(rows)[:, 0:1] / MODEL_WIDTH
    grad = (
        gradient[...].astype(F32) + column * scaled - entry[...].astype(F32) * factor
    ).astype(BF)
    slot = lax.broadcasted_iota(jnp.int32, (VIS, SEQ), 0)
    position = lax.broadcasted_iota(jnp.int32, (VIS, SEQ), 1)
    first = core[0] == 0
    above, below = grad[:SEQ, :], grad[SEQ:, :]
    for index, rows, out in (
        (core[0], jnp.where(first, above, below), own_slots),
        (1 - core[0], jnp.where(first, below, above), other_slots),
    ):
        inside = (position == starts[index] + slot) & (slot < counts[index] * TOKT)
        out[...] = nn(inside.astype(F32).astype(BF), rows).astype(BF)


def second_output_kernel(core, values, totals, weights, hidden, own_hidden, other_hidden):
    column = inverse_of(rows_to_columns(totals[...])[:, 0:1])
    value_rows = (values[...].astype(F32) * column).astype(BF)
    attended = attended_rows(weights, 1, value_rows)
    output = (hidden[...].astype(F32) + attended).astype(BF)
    first = core[0] == 0
    own_hidden[...] = jnp.where(first, hidden[...], output)
    other_hidden[...] = jnp.where(first, output, hidden[...])


def swap_cores(block):
    return lax.ppermute(block, "section", [(0, 1), (1, 0)])


def to_heads(block):
    return lax.all_to_all(block, ("section", "tp"), 0, 0)


def on_device(
    embeddings,
    visual,
    image_block_count,
    starts,
    lengths,
    queries,
    layer_key_vectors,
    input_norm_gain,
    frozen_value_weight,
    adapter_down_map,
    adapter_up_map,
    cotangent,
):
    section = lax.axis_index("section")
    tp = lax.axis_index("tp")
    n_fsdp = lax.axis_size("fsdp")
    n_y = n_fsdp // KVH
    core = jnp.stack([section, tp]).astype(jnp.int32)
    counts = image_block_count[:, 0]
    begins = starts[:, 0]
    seq_lengths = lengths[:, 0]

    shard = frozen_value_weight[0].T
    pieces = shard.reshape(shard.shape[0], 2, HALF).transpose(1, 0, 2)
    pieces = jnp.broadcast_to(pieces[:, None], (2, n_y) + pieces.shape[1:])
    pieces = pieces.reshape((2 * n_y,) + pieces.shape[2:])
    head_groups = [
        [s * n_fsdp + z * n_y + y for s in range(2) for y in range(n_y)] for z in range(KVH)
    ]
    head_columns = lax.all_to_all(
        pieces, ("section", "fsdp"), 0, 0, axis_index_groups=head_groups
    ).reshape(2, HD, HALF)
    row_groups = [[z * n_y + y for z in range(KVH)] for y in range(n_y)]
    columns = lax.all_gather(head_columns, "fsdp", axis=0, axis_index_groups=row_groups)

    own = (
        visual[0, 0],
        queries[0].reshape(ROWS, 2 * HALF),
        layer_key_vectors[0].reshape(ROWS, 2 * HD),
        adapter_down_map[0].T,
        adapter_up_map[0],
        jnp.broadcast_to(input_norm_gain, (RANK, 2 * HALF)),
    )
    (packed,) = call(pack_kernel, "pack", [((R_END, HALF), BF)], (core,), own)

    wide = ((ROWS, HALF), BF)
    low = ((RANK, ROWS), F32)
    sums = ((SUBLANES, ROWS), F32)
    maps = ((2, RANK, HALF), BF)
    blocks = ((PEERS, ROWS, HD), BF)
    mixed = ((PEERS, R_PAY, HD), BF)
    weights, entry, cotangent_half, downs, ups, gains, payload = call(
        prepare_kernel,
        "prepare",
        [((2, MB, HEADS * SEQ, SEQ), BF), wide, wide, maps, maps, maps, mixed],
        (core, counts, begins, seq_lengths),
        (swap_cores(packed), *own, embeddings, cotangent),
    )

    columns_0, columns_1 = columns[:, 0], columns[:, 1]

    normed_0, sums_0, adapter_0, full_gradient_1, own_gradient_1, lora_gradient_1 = call(
        entry_norm_kernel,
        "entry_norm",
        [wide, sums, low, wide, ((ROWS, HD), BF), low],
        (core,),
        (to_heads(payload), entry, ups, gains),
    )
    (partial_0,) = call(
        first_values_kernel, "values_0", [blocks], (), (normed_0, downs, ups, columns_0)
    )
    (scaled_1,) = call(
        scaled_kernel,
        "scaled_1",
        [wide],
        (),
        (full_gradient_1, lora_gradient_1, downs, gains, columns_1),
    )
    hidden_0, value_rows, payload, partial_1 = call(
        first_output_kernel,
        "first_output",
        [wide, ((ROWS, HD), F32), ((PEERS, SUBLANES, ROWS), F32), blocks],
        (),
        (to_heads(partial_0), weights, entry, scaled_1, gains, downs, ups, columns_1),
    )
    values_1 = lax.psum_scatter(partial_1, ("section", "tp"), scatter_dimension=0)
    gradient, totals, down_gradient_1, payload = call(
        first_gradient_kernel,
        "first_gradient",
        [
            wide,
            sums,
            ((RANK, HALF), F32),
            mixed,
        ],
        (),
        (
            to_heads(payload),
            hidden_0,
            scaled_1,
            cotangent_half,
            weights,
            value_rows,
            gains,
            downs,
            lora_gradient_1,
        ),
    )
    gathered = to_heads(payload)
    (chunks,) = call(
        map_gradient_kernel,
        "map_gradient",
        [((2 * n_y, M_ROWS, HD), F32)],
        (core,),
        (
            gathered,
            ups,
            adapter_0,
            totals,
            own_gradient_1,
            down_gradient_1,
            normed_0,
        ),
    )
    own_slots, other_slots = call(
        slot_gradient_kernel,
        "slot_gradient",
        [((VIS, HALF), BF)] * 2,
        (core, counts, begins),
        (gathered, ups, downs, gains, sums_0, columns_0, gradient, entry),
    )
    other_slots = swap_cores(other_slots)
    own_hidden, other_hidden = call(
        second_output_kernel, "second_output", [wide] * 2, (core,), (values_1, totals, weights, hidden_0)
    )
    other_hidden = swap_cores(other_hidden)

    halves_of_maps = ((8, 2, M_ROWS, HD), BF)
    near = lax.all_to_all(chunks, ("section", "fsdp"), 0, 0, axis_index_groups=head_groups)
    (near,) = call(
        near_sum_kernel, "near_sum", [halves_of_maps], (), (near,), after=(other_slots,)
    )
    far = lax.all_to_all(near, "fsdp", 0, 0, axis_index_groups=row_groups)
    (far,) = call(far_sum_kernel, "far_sum", [halves_of_maps], (), (far,))
    y_groups = [[z * n_y + y for y in range(n_y)] for z in range(KVH)]
    summed = lax.all_to_all(far, "fsdp", 0, 0, axis_index_groups=y_groups)

    in_vmem = pl.BlockSpec(memory_space=pltpu.VMEM)
    anywhere = pl.BlockSpec(memory_space=pl.ANY)
    hidden, slots, down_sum, up_sum = pl.pallas_call(
        functools.partial(finish_kernel, scale=1.0 / math.sqrt(MB * SEQ * n_fsdp)),
        out_shape=[
            jax.ShapeDtypeStruct((ROWS, 2 * HALF), BF),
            jax.ShapeDtypeStruct((VIS, 2 * HALF), BF),
            jax.ShapeDtypeStruct((RANK, 2 * HALF), F32),
            jax.ShapeDtypeStruct((RANK, 2 * HD), F32),
        ],
        in_specs=[pl.BlockSpec(memory_space=pltpu.SMEM), in_vmem] + [anywhere] * 4,
        out_specs=[anywhere, anywhere, in_vmem, in_vmem],
        scratch_shapes=[pltpu.SemaphoreType.DMA((4,))],
        name="finish",
    )(core, summed, own_hidden, other_hidden, own_slots, other_slots)
    return (
        hidden.reshape(1, MB, SEQ, 2 * HALF),
        slots[None, None],
        down_sum.T[None],
        up_sum[None],
    )


def solution(mesh):
    return jax.shard_map(
        on_device,
        mesh=mesh,
        in_specs=(
            P(None, "fsdp", "tp"),
            P("section", "fsdp", None, "tp"),
            P(None, "fsdp"),
            P(None, "fsdp"),
            P(None, "fsdp"),
            P("section", None, "fsdp", "tp"),
            P("section", None, "fsdp", "tp"),
            P("section", "tp"),
            P("section", "tp", "fsdp"),
            P("section", "tp", None),
            P("section", None, None),
            P(None, "fsdp", "tp"),
        ),
        out_specs=(
            P("section", None, "fsdp", "tp"),
            P("section", "fsdp", None, "tp"),
            P("section", "tp", None),
            P("section", None, "tp"),
        ),
        check_vma=False,
    )
```

```python
import functools
import math

import jax
import jax.numpy as jnp
from jax import lax
from jax.experimental import pallas as pl
from jax.experimental.pallas import tpu as pltpu
from jax.sharding import PartitionSpec as P

MODEL_WIDTH = 8192
HD = 128
TOKT = 32
ADAPTER_SCALE = 0.5
EPS = 1e-06

SEQ = 128
MB = 2
ROWS = MB * SEQ
VIS = 96
RANK = 16
HEADS = 8
HALF = HEADS * HD
KVH = 8
PEERS = 8
VMEM_BYTES = 40 * 1024 * 1024

BF = jnp.bfloat16
F32 = jnp.float32

R_VIS, R_Q, R_K, R_DN, R_UP, R_GN, R_END = 0, 96, 352, 384, 400, 416, 432
R_SUM, R_LOW, R_PAY = ROWS, ROWS + RANK, ROWS + RANK + 2 * RANK
SUBLANES = 8


def block_of(head):
    return (head % 2) * 4 + head // 2


def nt(left, right):
    return lax.dot_general(left, right, (((1,), (1,)), ((), ())), preferred_element_type=F32)


def tn(left, right):
    return lax.dot_general(left, right, (((0,), (0,)), ((), ())), preferred_element_type=F32)


def nn(left, right):
    return jnp.dot(left, right, preferred_element_type=F32)


def stack_heads(block):
    return jnp.concatenate([block[:, h * HD : (h + 1) * HD] for h in range(HEADS)], axis=0)


def unstack_heads(block):
    return jnp.concatenate([block[h * SEQ : (h + 1) * SEQ, :] for h in range(HEADS)], axis=1)


def columns_to_rows(*columns):
    lane = lax.broadcasted_iota(jnp.int32, (ROWS, HD), 1)
    square = jnp.zeros((ROWS, HD), F32)
    for at, column in enumerate(columns):
        square = jnp.where(lane == at, column, square)
    return square.T[:SUBLANES, :]


def rows_to_columns(rows):
    padded = jnp.concatenate([rows, jnp.zeros((HD - SUBLANES, ROWS), F32)], axis=0)
    return padded.T


def payload_block(values, column, low_rank):
    row = columns_to_rows(column)[0:1, :]
    high = row.astype(BF).astype(F32)
    low = row - high
    at = lax.broadcasted_iota(jnp.int32, (RANK, HD), 0)
    sums = jnp.zeros((RANK, HD), F32)
    for index, part in enumerate((high[:, :HD], high[:, HD:], low[:, :HD], low[:, HD:])):
        sums = jnp.where(at == index, part, sums)
    low_rank = low_rank.astype(BF)
    return jnp.concatenate(
        [values, sums.astype(BF), low_rank[:, :HD], low_rank[:, HD:]], axis=0
    )


def total_of_payloads(blocks):
    sums = blocks[0, R_SUM:R_LOW, :].astype(F32)
    low_rank = blocks[0, R_LOW:, :].astype(F32)
    for peer in range(1, PEERS):
        sums = sums + blocks[peer, R_SUM:R_LOW, :].astype(F32)
        low_rank = low_rank + blocks[peer, R_LOW:, :].astype(F32)
    left = sums[0:1, :] + sums[2:3, :]
    right = sums[1:2, :] + sums[3:4, :]
    row = jnp.concatenate([left, right], axis=1)
    at = lax.broadcasted_iota(jnp.int32, (SUBLANES, ROWS), 0)
    rows = jnp.where(at == 0, row, 0.0)
    return rows, jnp.concatenate([low_rank[:RANK, :], low_rank[RANK:, :]], axis=1)


def inverse_of(squares):
    return lax.rsqrt(squares / MODEL_WIDTH + EPS)


def pack_kernel(core, visual, queries, keys, down, up, gain, out):
    other = 1 - core[0]
    at = pl.multiple_of(other * HALF, HALF)
    key_at = pl.multiple_of(other * HD, HD)
    out[R_VIS:R_Q, :] = visual[:, pl.ds(at, HALF)]
    out[R_Q:R_K, :] = queries[:, pl.ds(at, HALF)]
    for j in range(8):
        out[R_K:R_DN, j * HD : (j + 1) * HD] = keys[j * 32 : (j + 1) * 32, pl.ds(key_at, HD)]
    out[R_DN:R_UP, :] = down[:, pl.ds(at, HALF)]
    out[R_UP:R_GN, :] = up[...]
    out[R_GN:R_END, :] = gain[:, pl.ds(at, HALF)]


def softmax_of(query_rows, key_rows, length):
    scores = nt(stack_heads(query_rows), key_rows) / math.sqrt(HD)
    shape = scores.shape
    row = lax.rem(lax.broadcasted_iota(jnp.int32, shape, 0), SEQ)
    column = lax.broadcasted_iota(jnp.int32, shape, 1)
    allowed = (column <= row) & (column < length)
    scores = jnp.where(allowed, scores, -jnp.inf)
    top = jnp.max(scores, axis=-1, keepdims=True)
    weights = jnp.exp(scores - top)
    return (weights / jnp.sum(weights, axis=-1, keepdims=True)).astype(BF)


def prepare_kernel(
    core, counts, starts, lengths,
    received, visual, queries, keys, down, up, gain, embeddings, cotangent,
    weights, entry, cotangent_half, downs, ups, gains, payload,
):
    own = core[0]
    other = 1 - own
    at = pl.multiple_of(own * HALF, HALF)
    key_at = pl.multiple_of(own * HD, HD)
    half = pl.ds(at, HALF)
    downs[own] = down[:, half]
    downs[other] = received[R_DN:R_UP, :]
    ups[own] = up[...]
    ups[other] = received[R_UP:R_GN, :]
    gains[own] = gain[:, half]
    gains[other] = received[R_GN:R_END, :]
    position = lax.broadcasted_iota(jnp.int32, (SEQ, VIS), 0)
    slot = lax.broadcasted_iota(jnp.int32, (SEQ, VIS), 1)
    place = lax.broadcasted_iota(jnp.int32, (SEQ, 1), 0)
    for index, table in ((own, visual[:, half]), (other, received[R_VIS:R_Q, :])):
        begin = starts[index]
        count = counts[index] * TOKT
        placing = ((position == begin + slot) & (slot < count)).astype(F32).astype(BF)
        inserted = nn(placing, table).astype(BF)
        covered = (place >= begin) & (place < begin + count)
        rows = pl.ds(pl.multiple_of(index * SEQ, SEQ), SEQ)
        entry[rows, :] = jnp.where(covered, inserted, embeddings[index, :, half])
    for m in range(MB):
        rows = slice(m * SEQ, (m + 1) * SEQ)
        cotangent_half[rows, :] = cotangent[m, :, half]
        weights[own, m] = softmax_of(queries[rows, half], keys[rows, pl.ds(key_at, HD)], lengths[m])
        other_keys = jnp.concatenate(
            [received[R_K:R_DN, j * HD : (j + 1) * HD] for j in range(4 * m, 4 * m + 4)], axis=0
        )
        weights[other, m] = softmax_of(
            received[R_Q + m * SEQ : R_Q + (m + 1) * SEQ, :], other_keys, lengths[m]
        )
    value_gradient = jnp.concatenate(
        [
            tn(weights[1, m], stack_heads(cotangent_half[m * SEQ : (m + 1) * SEQ, :]))
            for m in range(MB)
        ],
        axis=0,
    ).astype(BF)
    entry_float = entry[...].astype(F32)
    squares = jnp.sum(entry_float * entry_float, axis=-1, keepdims=True)
    gained = (entry_float * gains[0][0:1, :].astype(F32)).astype(BF)
    block = payload_block(value_gradient, squares, nt(downs[0], gained))
    for peer in range(PEERS):
        payload[peer] = block


def entry_norm_kernel(
    core, received, entry, ups, gains,
    normed, inverse, adapter_rows, full_gradient, own_gradient, lora_gradient,
):
    rows, low_rank = total_of_payloads(received)
    column = inverse_of(rows_to_columns(rows)[:, 0:1])
    inverse[...] = jnp.broadcast_to(column, (ROWS, HD))
    adapter_rows[...] = low_rank * inverse_of(rows[0:1, :])
    gain = gains[0][0:1, :].astype(F32)
    normed[...] = (entry[...].astype(F32) * column * gain).astype(BF)
    for head in range(KVH):
        full_gradient[:, head * HD : (head + 1) * HD] = received[block_of(head), :ROWS, :]
    own_gradient[...] = received[core[0] * 4 + core[1], :ROWS, :]
    lora_gradient[...] = ADAPTER_SCALE * nt(ups[1], full_gradient[...])


def values_kernel(layer, normed, columns, downs, ups, out):
    rows = normed[...]
    adapter = (ADAPTER_SCALE * nt(rows, downs[layer])).astype(BF)
    for pair in range(KVH // 2):
        weight = columns[2 * pair : 2 * pair + 2, layer].reshape(2 * HD, HALF)
        up = ups[layer][:, 2 * pair * HD : (2 * pair + 2) * HD]
        partial = (nt(rows, weight) + nn(adapter, up)).astype(BF)
        out[block_of(2 * pair)] = partial[:, :HD]
        out[block_of(2 * pair + 1)] = partial[:, HD:]


def scaled_kernel(full_gradient, lora_gradient, columns, downs, gains, scaled):
    weight = columns[:, 1].reshape(KVH * HD, HALF)
    grad = nn(full_gradient[...], weight) + tn(lora_gradient[...].astype(BF), downs[1])
    scaled[...] = grad * gains[1][0:1, :].astype(F32)


def attended_rows(weights, layer, value_rows):
    return jnp.concatenate(
        [
            unstack_heads(nn(weights[layer, m], value_rows[m * SEQ : (m + 1) * SEQ, :]))
            for m in range(MB)
        ],
        axis=0,
    )


def first_output_kernel(
    received, weights, entry, scaled, hidden, value_rows, payload
):
    values = received[0].astype(F32)
    for peer in range(1, PEERS):
        values = values + received[peer].astype(F32)
    value_rows[...] = values
    attended = attended_rows(weights, 0, values.astype(BF))
    output = (entry[...].astype(F32) + attended).astype(BF)
    hidden[...] = output
    output_float = output.astype(F32)
    squares = jnp.sum(output_float * output_float, axis=-1, keepdims=True)
    dots = jnp.sum(output_float * scaled[...], axis=-1, keepdims=True)
    block = columns_to_rows(squares, dots)
    for peer in range(PEERS):
        payload[peer] = block


def first_gradient_kernel(
    received, weights, hidden, scaled, cotangent_half, gains, downs, value_rows, lora_gradient,
    gradient, normed, inverse_row, down_gradient, payload,
):
    total = received[0]
    for peer in range(1, PEERS):
        total = total + received[peer]
    sums = rows_to_columns(total)
    column = inverse_of(sums[:, 0:1])
    factor = column * column * column * sums[:, 1:2] / MODEL_WIDTH
    inverse_row[...] = inverse_of(total)
    hidden_float = hidden[...].astype(F32)
    gained = hidden_float * gains[1][0:1, :].astype(F32)
    rows = (gained * column).astype(BF)
    normed[...] = rows
    down_gradient[...] = nn(lora_gradient[...].astype(BF), rows)
    grad = (
        cotangent_half[...].astype(F32) + column * scaled[...] - hidden_float * factor
    ).astype(BF)
    gradient[...] = grad
    value_gradient = jnp.concatenate(
        [tn(weights[0, m], stack_heads(grad[m * SEQ : (m + 1) * SEQ, :])) for m in range(MB)],
        axis=0,
    ).astype(BF)
    dots = jnp.sum(value_gradient.astype(F32) * value_rows[...], axis=-1, keepdims=True)
    block = payload_block(value_gradient, dots, nt(downs[1], gained.astype(BF)))
    for peer in range(PEERS):
        payload[peer] = block


def map_chunks(down_gradient, up_gradient):
    quarter = HALF // 4
    left = jnp.concatenate(
        [down_gradient[:, q * quarter : (q + 1) * quarter] for q in range(4)], axis=0
    )
    right = jnp.concatenate([up_gradient, jnp.zeros((3 * RANK, HD), F32)], axis=0)
    return jnp.concatenate([left, right], axis=1)


def gathered_gradient(received):
    return jnp.concatenate([received[block_of(head), :ROWS, :] for head in range(KVH)], axis=1)


def map_gradient_kernel(
    core, received, ups, normed_0, adapter_0, inverse_row, gradient_1, down_gradient_1, out
):
    _, low_rank = total_of_payloads(received)
    lora_0 = ADAPTER_SCALE * nt(ups[0], gathered_gradient(received))
    own = received[core[0] * 4 + core[1], :ROWS, :]
    down_0 = nn(lora_0.astype(BF), normed_0[...])
    up_0 = ADAPTER_SCALE * nn(adapter_0[...].astype(BF), own)
    adapter_1 = (low_rank * inverse_row[0:1, :]).astype(BF)
    up_1 = ADAPTER_SCALE * nn(adapter_1, gradient_1[...])
    chunks = (map_chunks(down_0, up_0), map_chunks(down_gradient_1[...], up_1))
    for layer in range(2):
        out[layer * 4 * RANK : (layer + 1) * 4 * RANK] = chunks[layer][:, None, :]


def slot_gradient_kernel(
    core, counts, starts, received, ups, columns, downs, gains, entry, inverse, gradient,
    own_slots, other_slots,
):
    dots, _ = total_of_payloads(received)
    full_gradient = gathered_gradient(received)
    lora_gradient = ADAPTER_SCALE * nt(ups[0], full_gradient)
    column = inverse[:, 0:1]
    factor = column * column * rows_to_columns(dots)[:, 0:1] / MODEL_WIDTH
    weight = columns[:, 0].reshape(KVH * HD, HALF)
    grad = nn(full_gradient, weight) + tn(lora_gradient.astype(BF), downs[0])
    scaled = grad * gains[0][0:1, :].astype(F32)
    rows = (
        gradient[...].astype(F32) + column * scaled - entry[...].astype(F32) * factor
    ).astype(BF)
    slot = lax.broadcasted_iota(jnp.int32, (VIS, SEQ), 0)
    position = lax.broadcasted_iota(jnp.int32, (VIS, SEQ), 1)
    first = core[0] == 0
    above, below = rows[:SEQ, :], rows[SEQ:, :]
    for index, block, out in (
        (core[0], jnp.where(first, above, below), own_slots),
        (1 - core[0], jnp.where(first, below, above), other_slots),
    ):
        inside = (position == starts[index] + slot) & (slot < counts[index] * TOKT)
        out[...] = nn(inside.astype(F32).astype(BF), block).astype(BF)


def second_output_kernel(core, values, weights, hidden, own_hidden, other_hidden):
    attended = attended_rows(weights, 1, values[...])
    output = (hidden[...].astype(F32) + attended).astype(BF)
    first = core[0] == 0
    own_hidden[...] = jnp.where(first, hidden[...], output)
    other_hidden[...] = jnp.where(first, output, hidden[...])


def sum_kernel(arrived, out, token):
    token[...] = jnp.zeros_like(token)
    n_fsdp = arrived.shape[0] // 2
    halves = [jnp.sum(arrived[h * n_fsdp : (h + 1) * n_fsdp], axis=0) for h in range(2)]
    row = jnp.concatenate(halves, axis=1)
    for at in range(n_fsdp):
        out[at] = row


def maps_kernel(arrived, down_sum, up_sum, *, scale):
    rows = arrived[...].reshape(4 * RANK, 2 * (HALF // 4 + HD)) * scale
    quarter, width = HALF // 4, HALF // 4 + HD
    for half in range(2):
        for q in range(4):
            to = half * HALF + q * quarter
            down_sum[:, to : to + quarter] = rows[
                q * RANK : (q + 1) * RANK, half * width : half * width + quarter
            ]
        up_sum[:, half * HD : (half + 1) * HD] = rows[
            :RANK, half * width + quarter : (half + 1) * width
        ]


def place_kernel(core, own, other, out, token):
    token[...] = jnp.zeros_like(token)
    at = pl.multiple_of(core[0] * HALF, HALF)
    out[:, pl.ds(at, HALF)] = own[...]
    out[:, pl.ds(HALF - at, HALF)] = other[...]


def call(kernel, name, results, scalars, arrays, after=()):
    n_read = len(scalars) + len(arrays)

    def body(*refs):
        kernel(*refs[:n_read], *refs[n_read + len(after) :])

    moved = sum(a.size * a.dtype.itemsize for a in arrays)
    moved += sum(math.prod(shape) * jnp.dtype(dtype).itemsize for shape, dtype in results)
    in_vmem = pl.BlockSpec(memory_space=pltpu.VMEM)
    return pl.pallas_call(
        body,
        out_shape=[jax.ShapeDtypeStruct(shape, dtype) for shape, dtype in results],
        in_specs=[pl.BlockSpec(memory_space=pltpu.SMEM)] * len(scalars)
        + [in_vmem] * len(arrays)
        + [pl.BlockSpec(memory_space=pl.ANY)] * len(after),
        out_specs=[in_vmem] * len(results),
        compiler_params=pltpu.CompilerParams(vmem_limit_bytes=VMEM_BYTES),
        cost_estimate=pl.CostEstimate(flops=0, bytes_accessed=moved, transcendentals=0),
        name=name,
    )(*scalars, *arrays, *after)


def swap_cores(block):
    return lax.ppermute(block, "section", [(0, 1), (1, 0)])


def to_heads(block):
    return lax.all_to_all(block, ("section", "tp"), 0, 0)


def on_device(
    embeddings,
    visual,
    image_block_count,
    starts,
    lengths,
    queries,
    layer_key_vectors,
    input_norm_gain,
    frozen_value_weight,
    adapter_down_map,
    adapter_up_map,
    cotangent,
):
    section = lax.axis_index("section")
    tp = lax.axis_index("tp")
    n_fsdp = lax.axis_size("fsdp")
    n_y = n_fsdp // KVH
    core = jnp.stack([section, tp]).astype(jnp.int32)
    counts = image_block_count[:, 0]
    begins = starts[:, 0]
    seq_lengths = lengths[:, 0]

    shard = frozen_value_weight[0].T
    pieces = shard.reshape(shard.shape[0], 2, HALF).transpose(1, 0, 2)
    pieces = jnp.broadcast_to(pieces[:, None], (2, n_y) + pieces.shape[1:])
    pieces = pieces.reshape((2 * n_y,) + pieces.shape[2:])
    head_groups = [
        [s * n_fsdp + z * n_y + y for s in range(2) for y in range(n_y)] for z in range(KVH)
    ]
    head_columns = lax.all_to_all(
        pieces, ("section", "fsdp"), 0, 0, axis_index_groups=head_groups
    ).reshape(2, HD, HALF)
    row_groups = [[z * n_y + y for z in range(KVH)] for y in range(n_y)]
    columns = lax.all_gather(head_columns, "fsdp", axis=0, axis_index_groups=row_groups)

    own_visual = visual[0, 0]
    own_queries = queries[0].reshape(ROWS, 2 * HALF)
    own_keys = layer_key_vectors[0].reshape(ROWS, 2 * HD)
    own_down = adapter_down_map[0].T
    own_up = adapter_up_map[0]
    own_gain = jnp.broadcast_to(input_norm_gain, (RANK, 2 * HALF))
    own = (own_visual, own_queries, own_keys, own_down, own_up, own_gain)
    (packed,) = call(pack_kernel, "pack", [((R_END, HALF), BF)], (core,), own)
    received = swap_cores(packed)

    wide = ((ROWS, HALF), BF)
    small = ((RANK, ROWS), F32)
    maps = ((2, RANK, HALF), BF)
    weights, entry, cotangent_half, downs, ups, gains, payload = call(
        prepare_kernel,
        "prepare",
        [
            ((2, MB, HEADS * SEQ, SEQ), BF),
            wide,
            wide,
            maps,
            maps,
            maps,
            ((PEERS, R_PAY, HD), BF),
        ],
        (core, counts, begins, seq_lengths),
        (received, *own, embeddings, cotangent),
    )
    normed_0, inverse_0, adapter_0, full_gradient, own_gradient_1, lora_gradient_1 = call(
        entry_norm_kernel,
        "entry_norm",
        [wide, ((ROWS, HD), F32), small, wide, ((ROWS, HD), BF), small],
        (core,),
        (to_heads(payload), entry, ups, gains),
    )

    blocks = ((PEERS, ROWS, HD), BF)
    (partial_0,) = call(
        functools.partial(values_kernel, 0), "values_0", [blocks], (), (normed_0, columns, downs, ups)
    )
    (scaled_1,) = call(
        scaled_kernel,
        "scaled_1",
        [((ROWS, HALF), F32)],
        (),
        (full_gradient, lora_gradient_1, columns, downs, gains),
    )
    hidden_0, value_rows, payload = call(
        first_output_kernel,
        "first_output",
        [wide, ((ROWS, HD), F32), ((PEERS, SUBLANES, ROWS), F32)],
        (),
        (to_heads(partial_0), weights, entry, scaled_1),
    )
    gradient, normed_1, inverse_row, down_gradient_1, payload = call(
        first_gradient_kernel,
        "first_gradient",
        [
            wide,
            wide,
            ((SUBLANES, ROWS), F32),
            ((RANK, HALF), F32),
            ((PEERS, R_PAY, HD), BF),
        ],
        (),
        (
            to_heads(payload),
            weights,
            hidden_0,
            scaled_1,
            cotangent_half,
            gains,
            downs,
            value_rows,
            lora_gradient_1,
        ),
    )
    gathered = to_heads(payload)
    (partial_1,) = call(
        functools.partial(values_kernel, 1), "values_1", [blocks], (), (normed_1, columns, downs, ups)
    )
    values_1 = lax.psum_scatter(partial_1, ("section", "tp"), scatter_dimension=0)

    (chunks,) = call(
        map_gradient_kernel,
        "map_gradient",
        [((2 * n_fsdp, 1, HALF // 4 + HD), F32)],
        (core,),
        (gathered, ups, normed_0, adapter_0, inverse_row, own_gradient_1, down_gradient_1),
    )
    width = HALF // 4 + HD
    arrived = lax.all_to_all(chunks, ("section", "fsdp"), 0, 0)
    token = ((SUBLANES, HD), F32)
    summed, summed_token = call(
        sum_kernel, "sum_maps", [((n_fsdp, 1, 2 * width), F32), token], (), (arrived,)
    )
    everywhere = lax.all_to_all(summed, "fsdp", 0, 0)

    own_slots, other_slots = call(
        slot_gradient_kernel,
        "slot_gradient",
        [((VIS, HALF), BF)] * 2,
        (core, counts, begins),
        (gathered, ups, columns, downs, gains, entry, inverse_0, gradient),
    )
    own_hidden, other_hidden = call(
        second_output_kernel,
        "second_output",
        [wide] * 2,
        (core,),
        (values_1, weights, hidden_0),
        after=(summed_token,),
    )
    slots, slots_placed = call(
        place_kernel,
        "place_slots",
        [((VIS, 2 * HALF), BF), token],
        (core,),
        (own_slots, swap_cores(other_slots)),
    )
    hidden, hidden_placed = call(
        place_kernel,
        "place_hidden",
        [((ROWS, 2 * HALF), BF), token],
        (core,),
        (own_hidden, swap_cores(other_hidden)),
    )
    down_sum, up_sum = call(
        functools.partial(maps_kernel, scale=1.0 / math.sqrt(MB * SEQ * n_fsdp)),
        "maps",
        [((RANK, 2 * HALF), F32), ((RANK, 2 * HD), F32)],
        (),
        (everywhere,),
        after=(slots_placed, hidden_placed),
    )
    return (
        hidden.reshape(1, MB, SEQ, 2 * HALF),
        slots[None, None],
        down_sum.T[None],
        up_sum[None],
    )


def solution(mesh):
    return jax.shard_map(
        on_device,
        mesh=mesh,
        in_specs=(
            P(None, "fsdp", "tp"),
            P("section", "fsdp", None, "tp"),
            P(None, "fsdp"),
            P(None, "fsdp"),
            P(None, "fsdp"),
            P("section", None, "fsdp", "tp"),
            P("section", None, "fsdp", "tp"),
            P("section", "tp"),
            P("section", "tp", "fsdp"),
            P("section", "tp", None),
            P("section", None, None),
            P(None, "fsdp", "tp"),
        ),
        out_specs=(
            P("section", None, "fsdp", "tp"),
            P("section", "fsdp", None, "tp"),
            P("section", "tp", None),
            P("section", None, "tp"),
        ),
        check_vma=False,
    )
```

```python
import functools
import math

import jax
import jax.numpy as jnp
from jax import lax
from jax.experimental import pallas as pl
from jax.experimental.pallas import tpu as pltpu
from jax.sharding import PartitionSpec as P

MODEL_WIDTH = 8192
HD = 128
TOKT = 32
ADAPTER_SCALE = 0.5
EPS = 1e-06

SEQ = 128
MB = 2
ROWS = MB * SEQ
VIS = 96
RANK = 16
HEADS = 8
HALF = HEADS * HD
KVH = 8
PEERS = 8
VMEM_BYTES = 40 * 1024 * 1024

BF = jnp.bfloat16
F32 = jnp.float32

R_VIS, R_Q, R_K, R_DN, R_UP, R_GN, R_END = 0, 96, 352, 384, 400, 416, 432
R_SUM, R_LOW, R_PAY = ROWS, ROWS + RANK, ROWS + RANK + 2 * RANK
SUBLANES = 8


def block_of(head):
    return (head % 2) * 4 + head // 2


def nt(left, right):
    return lax.dot_general(left, right, (((1,), (1,)), ((), ())), preferred_element_type=F32)


def tn(left, right):
    return lax.dot_general(left, right, (((0,), (0,)), ((), ())), preferred_element_type=F32)


def nn(left, right):
    return jnp.dot(left, right, preferred_element_type=F32)


def stack_heads(block):
    return jnp.concatenate([block[:, h * HD : (h + 1) * HD] for h in range(HEADS)], axis=0)


def unstack_heads(block):
    return jnp.concatenate([block[h * SEQ : (h + 1) * SEQ, :] for h in range(HEADS)], axis=1)


def columns_to_rows(*columns):
    lane = lax.broadcasted_iota(jnp.int32, (ROWS, HD), 1)
    square = jnp.zeros((ROWS, HD), F32)
    for at, column in enumerate(columns):
        square = jnp.where(lane == at, column, square)
    return square.T[:SUBLANES, :]


def rows_to_columns(rows):
    padded = jnp.concatenate([rows, jnp.zeros((HD - SUBLANES, ROWS), F32)], axis=0)
    return padded.T


def payload_block(values, column, low_rank):
    row = columns_to_rows(column)[0:1, :]
    high = row.astype(BF).astype(F32)
    low = row - high
    at = lax.broadcasted_iota(jnp.int32, (RANK, HD), 0)
    sums = jnp.zeros((RANK, HD), F32)
    for index, part in enumerate((high[:, :HD], high[:, HD:], low[:, :HD], low[:, HD:])):
        sums = jnp.where(at == index, part, sums)
    low_rank = low_rank.astype(BF)
    return jnp.concatenate(
        [values, sums.astype(BF), low_rank[:, :HD], low_rank[:, HD:]], axis=0
    )


def total_of_payloads(blocks):
    sums = blocks[0, R_SUM:R_LOW, :].astype(F32)
    low_rank = blocks[0, R_LOW:, :].astype(F32)
    for peer in range(1, PEERS):
        sums = sums + blocks[peer, R_SUM:R_LOW, :].astype(F32)
        low_rank = low_rank + blocks[peer, R_LOW:, :].astype(F32)
    left = sums[0:1, :] + sums[2:3, :]
    right = sums[1:2, :] + sums[3:4, :]
    row = jnp.concatenate([left, right], axis=1)
    at = lax.broadcasted_iota(jnp.int32, (SUBLANES, ROWS), 0)
    rows = jnp.where(at == 0, row, 0.0)
    return rows, jnp.concatenate([low_rank[:RANK, :], low_rank[RANK:, :]], axis=1)


def inverse_of(squares):
    return lax.rsqrt(squares / MODEL_WIDTH + EPS)


def pack_kernel(core, visual, queries, keys, down, up, gain, out):
    other = 1 - core[0]
    at = pl.multiple_of(other * HALF, HALF)
    key_at = pl.multiple_of(other * HD, HD)
    out[R_VIS:R_Q, :] = visual[:, pl.ds(at, HALF)]
    out[R_Q:R_K, :] = queries[:, pl.ds(at, HALF)]
    for j in range(8):
        out[R_K:R_DN, j * HD : (j + 1) * HD] = keys[j * 32 : (j + 1) * 32, pl.ds(key_at, HD)]
    out[R_DN:R_UP, :] = down[:, pl.ds(at, HALF)]
    out[R_UP:R_GN, :] = up[...]
    out[R_GN:R_END, :] = gain[:, pl.ds(at, HALF)]


def softmax_of(query_rows, key_rows, length):
    scores = nt(stack_heads(query_rows), key_rows) / math.sqrt(HD)
    shape = scores.shape
    row = lax.rem(lax.broadcasted_iota(jnp.int32, shape, 0), SEQ)
    column = lax.broadcasted_iota(jnp.int32, shape, 1)
    allowed = (column <= row) & (column < length)
    scores = jnp.where(allowed, scores, -jnp.inf)
    top = jnp.max(scores, axis=-1, keepdims=True)
    weights = jnp.exp(scores - top)
    return (weights / jnp.sum(weights, axis=-1, keepdims=True)).astype(BF)


def prepare_kernel(
    core, counts, starts, lengths,
    received, visual, queries, keys, down, up, gain, embeddings, cotangent,
    weights, entry, cotangent_half, downs, ups, gains, payload,
):
    own = core[0]
    other = 1 - own
    at = pl.multiple_of(own * HALF, HALF)
    key_at = pl.multiple_of(own * HD, HD)
    half = pl.ds(at, HALF)
    downs[own] = down[:, half]
    downs[other] = received[R_DN:R_UP, :]
    ups[own] = up[...]
    ups[other] = received[R_UP:R_GN, :]
    gains[own] = gain[:, half]
    gains[other] = received[R_GN:R_END, :]
    position = lax.broadcasted_iota(jnp.int32, (SEQ, VIS), 0)
    slot = lax.broadcasted_iota(jnp.int32, (SEQ, VIS), 1)
    place = lax.broadcasted_iota(jnp.int32, (SEQ, 1), 0)
    for index, table in ((own, visual[:, half]), (other, received[R_VIS:R_Q, :])):
        begin = starts[index]
        count = counts[index] * TOKT
        placing = ((position == begin + slot) & (slot < count)).astype(F32).astype(BF)
        inserted = nn(placing, table).astype(BF)
        covered = (place >= begin) & (place < begin + count)
        rows = pl.ds(pl.multiple_of(index * SEQ, SEQ), SEQ)
        entry[rows, :] = jnp.where(covered, inserted, embeddings[index, :, half])
    for m in range(MB):
        rows = slice(m * SEQ, (m + 1) * SEQ)
        cotangent_half[rows, :] = cotangent[m, :, half]
        weights[own, m] = softmax_of(queries[rows, half], keys[rows, pl.ds(key_at, HD)], lengths[m])
        other_keys = jnp.concatenate(
            [received[R_K:R_DN, j * HD : (j + 1) * HD] for j in range(4 * m, 4 * m + 4)], axis=0
        )
        weights[other, m] = softmax_of(
            received[R_Q + m * SEQ : R_Q + (m + 1) * SEQ, :], other_keys, lengths[m]
        )
    value_gradient = jnp.concatenate(
        [
            tn(weights[1, m], stack_heads(cotangent_half[m * SEQ : (m + 1) * SEQ, :]))
            for m in range(MB)
        ],
        axis=0,
    ).astype(BF)
    entry_float = entry[...].astype(F32)
    squares = jnp.sum(entry_float * entry_float, axis=-1, keepdims=True)
    gained = (entry_float * gains[0][0:1, :].astype(F32)).astype(BF)
    block = payload_block(value_gradient, squares, nt(downs[0], gained))
    for peer in range(PEERS):
        payload[peer] = block


def entry_norm_kernel(
    core, received, entry, ups, gains,
    normed, inverse, adapter_rows, full_gradient, own_gradient, lora_gradient,
):
    rows, low_rank = total_of_payloads(received)
    column = inverse_of(rows_to_columns(rows)[:, 0:1])
    inverse[...] = jnp.broadcast_to(column, (ROWS, HD))
    adapter_rows[...] = low_rank * inverse_of(rows[0:1, :])
    gain = gains[0][0:1, :].astype(F32)
    normed[...] = (entry[...].astype(F32) * column * gain).astype(BF)
    for head in range(KVH):
        full_gradient[:, head * HD : (head + 1) * HD] = received[block_of(head), :ROWS, :]
    own_gradient[...] = received[core[0] * 4 + core[1], :ROWS, :]
    lora_gradient[...] = ADAPTER_SCALE * nt(ups[1], full_gradient[...])


def values_kernel(layer, normed, columns, downs, ups, out):
    rows = normed[...]
    adapter = (ADAPTER_SCALE * nt(rows, downs[layer])).astype(BF)
    for pair in range(KVH // 2):
        weight = columns[2 * pair : 2 * pair + 2, layer].reshape(2 * HD, HALF)
        up = ups[layer][:, 2 * pair * HD : (2 * pair + 2) * HD]
        partial = (nt(rows, weight) + nn(adapter, up)).astype(BF)
        out[block_of(2 * pair)] = partial[:, :HD]
        out[block_of(2 * pair + 1)] = partial[:, HD:]


def scaled_kernel(full_gradient, lora_gradient, columns, downs, gains, scaled):
    weight = columns[:, 1].reshape(KVH * HD, HALF)
    grad = nn(full_gradient[...], weight) + tn(lora_gradient[...].astype(BF), downs[1])
    scaled[...] = grad * gains[1][0:1, :].astype(F32)


def attended_rows(weights, layer, value_rows):
    return jnp.concatenate(
        [
            unstack_heads(nn(weights[layer, m], value_rows[m * SEQ : (m + 1) * SEQ, :]))
            for m in range(MB)
        ],
        axis=0,
    )


def first_output_kernel(
    received, weights, entry, scaled, hidden, value_rows, payload
):
    values = received[0].astype(F32)
    for peer in range(1, PEERS):
        values = values + received[peer].astype(F32)
    value_rows[...] = values
    attended = attended_rows(weights, 0, values.astype(BF))
    output = (entry[...].astype(F32) + attended).astype(BF)
    hidden[...] = output
    output_float = output.astype(F32)
    squares = jnp.sum(output_float * output_float, axis=-1, keepdims=True)
    dots = jnp.sum(output_float * scaled[...], axis=-1, keepdims=True)
    block = columns_to_rows(squares, dots)
    for peer in range(PEERS):
        payload[peer] = block


def first_gradient_kernel(
    received, weights, hidden, scaled, cotangent_half, gains, downs, value_rows, lora_gradient,
    gradient, normed, kept, payload,
):
    total = received[0]
    for peer in range(1, PEERS):
        total = total + received[peer]
    sums = rows_to_columns(total)
    column = inverse_of(sums[:, 0:1])
    factor = column * column * column * sums[:, 1:2] / MODEL_WIDTH
    hidden_float = hidden[...].astype(F32)
    gained = hidden_float * gains[1][0:1, :].astype(F32)
    rows = (gained * column).astype(BF)
    normed[...] = rows
    kept[:RANK, :] = nn(lora_gradient[...].astype(BF), rows)
    kept[RANK:, :ROWS] = inverse_of(total)
    kept[RANK:, ROWS:] = jnp.zeros((SUBLANES, HALF - ROWS), F32)
    grad = (
        cotangent_half[...].astype(F32) + column * scaled[...] - hidden_float * factor
    ).astype(BF)
    gradient[...] = grad
    value_gradient = jnp.concatenate(
        [tn(weights[0, m], stack_heads(grad[m * SEQ : (m + 1) * SEQ, :])) for m in range(MB)],
        axis=0,
    ).astype(BF)
    dots = jnp.sum(value_gradient.astype(F32) * value_rows[...], axis=-1, keepdims=True)
    block = payload_block(value_gradient, dots, nt(downs[1], gained.astype(BF)))
    for peer in range(PEERS):
        payload[peer] = block


def map_chunks(down_gradient, up_gradient):
    quarter = HALF // 4
    left = jnp.concatenate(
        [down_gradient[:, q * quarter : (q + 1) * quarter] for q in range(4)], axis=0
    )
    right = jnp.concatenate([up_gradient, jnp.zeros((3 * RANK, HD), F32)], axis=0)
    return jnp.concatenate([left, right], axis=1)


def gathered_gradient(received):
    return jnp.concatenate([received[block_of(head), :ROWS, :] for head in range(KVH)], axis=1)


def map_gradient_kernel(
    core, received, ups, normed_0, adapter_0, gradient_1, kept, out
):
    _, low_rank = total_of_payloads(received)
    lora_0 = ADAPTER_SCALE * nt(ups[0], gathered_gradient(received))
    own = received[core[0] * 4 + core[1], :ROWS, :]
    down_0 = nn(lora_0.astype(BF), normed_0[...])
    up_0 = ADAPTER_SCALE * nn(adapter_0[...].astype(BF), own)
    adapter_1 = (low_rank * kept[RANK : RANK + 1, :ROWS]).astype(BF)
    up_1 = ADAPTER_SCALE * nn(adapter_1, gradient_1[...])
    chunks = (map_chunks(down_0, up_0), map_chunks(kept[:RANK, :], up_1))
    for layer in range(2):
        out[layer * 4 * RANK : (layer + 1) * 4 * RANK] = chunks[layer][:, None, :]


def slot_gradient_kernel(
    core, counts, starts, received, ups, columns, downs, gains, entry, inverse, gradient,
    own_slots, other_slots,
):
    dots, _ = total_of_payloads(received)
    full_gradient = gathered_gradient(received)
    lora_gradient = ADAPTER_SCALE * nt(ups[0], full_gradient)
    column = inverse[:, 0:1]
    factor = column * column * rows_to_columns(dots)[:, 0:1] / MODEL_WIDTH
    weight = columns[:, 0].reshape(KVH * HD, HALF)
    grad = nn(full_gradient, weight) + tn(lora_gradient.astype(BF), downs[0])
    scaled = grad * gains[0][0:1, :].astype(F32)
    rows = (
        gradient[...].astype(F32) + column * scaled - entry[...].astype(F32) * factor
    ).astype(BF)
    slot = lax.broadcasted_iota(jnp.int32, (VIS, SEQ), 0)
    position = lax.broadcasted_iota(jnp.int32, (VIS, SEQ), 1)
    first = core[0] == 0
    above, below = rows[:SEQ, :], rows[SEQ:, :]
    for index, block, out in (
        (core[0], jnp.where(first, above, below), own_slots),
        (1 - core[0], jnp.where(first, below, above), other_slots),
    ):
        inside = (position == starts[index] + slot) & (slot < counts[index] * TOKT)
        out[...] = nn(inside.astype(F32).astype(BF), block).astype(BF)


def second_output_kernel(core, values, weights, hidden, own_hidden, other_hidden):
    attended = attended_rows(weights, 1, values[...])
    output = (hidden[...].astype(F32) + attended).astype(BF)
    first = core[0] == 0
    own_hidden[...] = jnp.where(first, hidden[...], output)
    other_hidden[...] = jnp.where(first, output, hidden[...])


def sum_kernel(arrived, out, token):
    token[...] = jnp.zeros_like(token)
    n_fsdp = arrived.shape[0] // 2
    halves = [jnp.sum(arrived[h * n_fsdp : (h + 1) * n_fsdp], axis=0) for h in range(2)]
    row = jnp.concatenate(halves, axis=1)
    for at in range(n_fsdp):
        out[at] = row


def maps_kernel(arrived, down_sum, up_sum, *, scale):
    rows = arrived[...].reshape(4 * RANK, 2 * (HALF // 4 + HD)) * scale
    quarter, width = HALF // 4, HALF // 4 + HD
    for half in range(2):
        for q in range(4):
            to = half * HALF + q * quarter
            down_sum[:, to : to + quarter] = rows[
                q * RANK : (q + 1) * RANK, half * width : half * width + quarter
            ]
        up_sum[:, half * HD : (half + 1) * HD] = rows[
            :RANK, half * width + quarter : (half + 1) * width
        ]


def place_kernel(core, own, other, out, token):
    token[...] = jnp.zeros_like(token)
    at = pl.multiple_of(core[0] * HALF, HALF)
    out[:, pl.ds(at, HALF)] = own[...]
    out[:, pl.ds(HALF - at, HALF)] = other[...]


def call(kernel, name, results, scalars, arrays, after=()):
    n_read = len(scalars) + len(arrays)

    def body(*refs):
        kernel(*refs[:n_read], *refs[n_read + len(after) :])

    moved = sum(a.size * a.dtype.itemsize for a in arrays)
    moved += sum(math.prod(shape) * jnp.dtype(dtype).itemsize for shape, dtype in results)
    in_vmem = pl.BlockSpec(memory_space=pltpu.VMEM)
    return pl.pallas_call(
        body,
        out_shape=[jax.ShapeDtypeStruct(shape, dtype) for shape, dtype in results],
        in_specs=[pl.BlockSpec(memory_space=pltpu.SMEM)] * len(scalars)
        + [in_vmem] * len(arrays)
        + [pl.BlockSpec(memory_space=pl.ANY)] * len(after),
        out_specs=[in_vmem] * len(results),
        compiler_params=pltpu.CompilerParams(vmem_limit_bytes=VMEM_BYTES),
        cost_estimate=pl.CostEstimate(flops=0, bytes_accessed=moved, transcendentals=0),
        name=name,
    )(*scalars, *arrays, *after)


def swap_cores(block):
    return lax.ppermute(block, "section", [(0, 1), (1, 0)])


def to_heads(block):
    return lax.all_to_all(block, ("section", "tp"), 0, 0)


def on_device(
    embeddings,
    visual,
    image_block_count,
    starts,
    lengths,
    queries,
    layer_key_vectors,
    input_norm_gain,
    frozen_value_weight,
    adapter_down_map,
    adapter_up_map,
    cotangent,
):
    section = lax.axis_index("section")
    tp = lax.axis_index("tp")
    n_fsdp = lax.axis_size("fsdp")
    n_y = n_fsdp // KVH
    core = jnp.stack([section, tp]).astype(jnp.int32)
    counts = image_block_count[:, 0]
    begins = starts[:, 0]
    seq_lengths = lengths[:, 0]

    shard = frozen_value_weight[0].T
    pieces = shard.reshape(shard.shape[0], 2, HALF).transpose(1, 0, 2)
    pieces = jnp.broadcast_to(pieces[:, None], (2, n_y) + pieces.shape[1:])
    pieces = pieces.reshape((2 * n_y,) + pieces.shape[2:])
    head_groups = [
        [s * n_fsdp + z * n_y + y for s in range(2) for y in range(n_y)] for z in range(KVH)
    ]
    head_columns = lax.all_to_all(
        pieces, ("section", "fsdp"), 0, 0, axis_index_groups=head_groups
    ).reshape(2, HD, HALF)
    row_groups = [[z * n_y + y for z in range(KVH)] for y in range(n_y)]
    columns = lax.all_gather(head_columns, "fsdp", axis=0, axis_index_groups=row_groups)

    own_visual = visual[0, 0]
    own_queries = queries[0].reshape(ROWS, 2 * HALF)
    own_keys = layer_key_vectors[0].reshape(ROWS, 2 * HD)
    own_down = adapter_down_map[0].T
    own_up = adapter_up_map[0]
    own_gain = jnp.broadcast_to(input_norm_gain, (RANK, 2 * HALF))
    own = (own_visual, own_queries, own_keys, own_down, own_up, own_gain)
    (packed,) = call(pack_kernel, "pack", [((R_END, HALF), BF)], (core,), own)
    received = swap_cores(packed)

    wide = ((ROWS, HALF), BF)
    small = ((RANK, ROWS), F32)
    maps = ((2, RANK, HALF), BF)
    weights, entry, cotangent_half, downs, ups, gains, payload = call(
        prepare_kernel,
        "prepare",
        [
            ((2, MB, HEADS * SEQ, SEQ), BF),
            wide,
            wide,
            maps,
            maps,
            maps,
            ((PEERS, R_PAY, HD), BF),
        ],
        (core, counts, begins, seq_lengths),
        (received, *own, embeddings, cotangent),
    )
    normed_0, inverse_0, adapter_0, full_gradient, own_gradient_1, lora_gradient_1 = call(
        entry_norm_kernel,
        "entry_norm",
        [wide, ((ROWS, HD), F32), small, wide, ((ROWS, HD), BF), small],
        (core,),
        (to_heads(payload), entry, ups, gains),
    )

    blocks = ((PEERS, ROWS, HD), BF)
    (partial_0,) = call(
        functools.partial(values_kernel, 0), "values_0", [blocks], (), (normed_0, columns, downs, ups)
    )
    (scaled_1,) = call(
        scaled_kernel,
        "scaled_1",
        [((ROWS, HALF), F32)],
        (),
        (full_gradient, lora_gradient_1, columns, downs, gains),
    )
    hidden_0, value_rows, payload = call(
        first_output_kernel,
        "first_output",
        [wide, ((ROWS, HD), F32), ((PEERS, SUBLANES, ROWS), F32)],
        (),
        (to_heads(partial_0), weights, entry, scaled_1),
    )
    gradient, normed_1, kept, payload = call(
        first_gradient_kernel,
        "first_gradient",
        [
            wide,
            wide,
            ((RANK + SUBLANES, HALF), F32),
            ((PEERS, R_PAY, HD), BF),
        ],
        (),
        (
            to_heads(payload),
            weights,
            hidden_0,
            scaled_1,
            cotangent_half,
            gains,
            downs,
            value_rows,
            lora_gradient_1,
        ),
    )
    gathered = to_heads(payload)
    (partial_1,) = call(
        functools.partial(values_kernel, 1), "values_1", [blocks], (), (normed_1, columns, downs, ups)
    )
    values_1 = lax.psum_scatter(partial_1, ("section", "tp"), scatter_dimension=0)

    (chunks,) = call(
        map_gradient_kernel,
        "map_gradient",
        [((2 * n_fsdp, 1, HALF // 4 + HD), F32)],
        (core,),
        (gathered, ups, normed_0, adapter_0, own_gradient_1, kept),
    )
    width = HALF // 4 + HD
    arrived = lax.all_to_all(chunks, ("section", "fsdp"), 0, 0)
    token = ((SUBLANES, HD), F32)
    summed, summed_token = call(
        sum_kernel, "sum_maps", [((n_fsdp, 1, 2 * width), F32), token], (), (arrived,)
    )
    everywhere = lax.all_to_all(summed, "fsdp", 0, 0)

    own_slots, other_slots = call(
        slot_gradient_kernel,
        "slot_gradient",
        [((VIS, HALF), BF)] * 2,
        (core, counts, begins),
        (gathered, ups, columns, downs, gains, entry, inverse_0, gradient),
    )
    own_hidden, other_hidden = call(
        second_output_kernel,
        "second_output",
        [wide] * 2,
        (core,),
        (values_1, weights, hidden_0),
    )
    slots, slots_placed = call(
        place_kernel,
        "place_slots",
        [((VIS, 2 * HALF), BF), token],
        (core,),
        (own_slots, swap_cores(other_slots)),
    )
    hidden, hidden_placed = call(
        place_kernel,
        "place_hidden",
        [((ROWS, 2 * HALF), BF), token],
        (core,),
        (own_hidden, swap_cores(other_hidden)),
    )
    down_sum, up_sum = call(
        functools.partial(maps_kernel, scale=1.0 / math.sqrt(MB * SEQ * n_fsdp)),
        "maps",
        [((RANK, 2 * HALF), F32), ((RANK, 2 * HD), F32)],
        (),
        (everywhere,),
        after=(slots_placed, hidden_placed),
    )
    return (
        hidden.reshape(1, MB, SEQ, 2 * HALF),
        slots[None, None],
        down_sum.T[None],
        up_sum[None],
    )


def solution(mesh):
    return jax.shard_map(
        on_device,
        mesh=mesh,
        in_specs=(
            P(None, "fsdp", "tp"),
            P("section", "fsdp", None, "tp"),
            P(None, "fsdp"),
            P(None, "fsdp"),
            P(None, "fsdp"),
            P("section", None, "fsdp", "tp"),
            P("section", None, "fsdp", "tp"),
            P("section", "tp"),
            P("section", "tp", "fsdp"),
            P("section", "tp", None),
            P("section", None, None),
            P(None, "fsdp", "tp"),
        ),
        out_specs=(
            P("section", None, "fsdp", "tp"),
            P("section", "fsdp", None, "tp"),
            P("section", "tp", None),
            P("section", None, "tp"),
        ),
        check_vma=False,
    )
```

```python
import functools
import math

import jax
import jax.numpy as jnp
from jax import lax
from jax.experimental import pallas as pl
from jax.experimental.pallas import tpu as pltpu
from jax.sharding import PartitionSpec as P

MODEL_WIDTH = 8192
HD = 128
TOKT = 32
ADAPTER_SCALE = 0.5
EPS = 1e-06

SEQ = 128
MB = 2
ROWS = MB * SEQ
VIS = 96
RANK = 16
HEADS = 8
HALF = HEADS * HD
KVH = 8
PEERS = 8
VMEM_BYTES = 40 * 1024 * 1024

BF = jnp.bfloat16
F32 = jnp.float32

R_VIS, R_Q, R_K, R_DN, R_UP, R_GN, R_END = 0, 96, 352, 384, 400, 416, 432
R_SUM, R_LOW, R_PAY = ROWS, ROWS + RANK, ROWS + RANK + 2 * RANK
SUBLANES = 8


def block_of(head):
    return (head % 2) * 4 + head // 2


def nt(left, right):
    return lax.dot_general(left, right, (((1,), (1,)), ((), ())), preferred_element_type=F32)


def tn(left, right):
    return lax.dot_general(left, right, (((0,), (0,)), ((), ())), preferred_element_type=F32)


def nn(left, right):
    return jnp.dot(left, right, preferred_element_type=F32)


def stack_heads(block):
    return jnp.concatenate([block[:, h * HD : (h + 1) * HD] for h in range(HEADS)], axis=0)


def unstack_heads(block):
    return jnp.concatenate([block[h * SEQ : (h + 1) * SEQ, :] for h in range(HEADS)], axis=1)


def columns_to_rows(*columns):
    lane = lax.broadcasted_iota(jnp.int32, (ROWS, HD), 1)
    square = jnp.zeros((ROWS, HD), F32)
    for at, column in enumerate(columns):
        square = jnp.where(lane == at, column, square)
    return square.T[:SUBLANES, :]


def rows_to_columns(rows):
    padded = jnp.concatenate([rows, jnp.zeros((HD - SUBLANES, ROWS), F32)], axis=0)
    return padded.T


def payload_block(values, column, low_rank):
    row = columns_to_rows(column)[0:1, :]
    high = row.astype(BF).astype(F32)
    low = row - high
    at = lax.broadcasted_iota(jnp.int32, (RANK, HD), 0)
    sums = jnp.zeros((RANK, HD), F32)
    for index, part in enumerate((high[:, :HD], high[:, HD:], low[:, :HD], low[:, HD:])):
        sums = jnp.where(at == index, part, sums)
    low_rank = low_rank.astype(BF)
    return jnp.concatenate(
        [values, sums.astype(BF), low_rank[:, :HD], low_rank[:, HD:]], axis=0
    )


def total_of_payloads(blocks):
    sums = blocks[0, R_SUM:R_LOW, :].astype(F32)
    low_rank = blocks[0, R_LOW:, :].astype(F32)
    for peer in range(1, PEERS):
        sums = sums + blocks[peer, R_SUM:R_LOW, :].astype(F32)
        low_rank = low_rank + blocks[peer, R_LOW:, :].astype(F32)
    left = sums[0:1, :] + sums[2:3, :]
    right = sums[1:2, :] + sums[3:4, :]
    row = jnp.concatenate([left, right], axis=1)
    at = lax.broadcasted_iota(jnp.int32, (SUBLANES, ROWS), 0)
    rows = jnp.where(at == 0, row, 0.0)
    return rows, jnp.concatenate([low_rank[:RANK, :], low_rank[RANK:, :]], axis=1)


def inverse_of(squares):
    return lax.rsqrt(squares / MODEL_WIDTH + EPS)


def pack_kernel(core, visual, queries, keys, down, up, gain, out):
    other = 1 - core[0]
    at = pl.multiple_of(other * HALF, HALF)
    key_at = pl.multiple_of(other * HD, HD)
    out[R_VIS:R_Q, :] = visual[:, pl.ds(at, HALF)]
    out[R_Q:R_K, :] = queries[:, pl.ds(at, HALF)]
    for j in range(8):
        out[R_K:R_DN, j * HD : (j + 1) * HD] = keys[j * 32 : (j + 1) * 32, pl.ds(key_at, HD)]
    out[R_DN:R_UP, :] = down[:, pl.ds(at, HALF)]
    out[R_UP:R_GN, :] = up[...]
    out[R_GN:R_END, :] = gain[:, pl.ds(at, HALF)]


def softmax_of(query_rows, key_rows, length):
    scores = nt(stack_heads(query_rows), key_rows) / math.sqrt(HD)
    shape = scores.shape
    row = lax.rem(lax.broadcasted_iota(jnp.int32, shape, 0), SEQ)
    column = lax.broadcasted_iota(jnp.int32, shape, 1)
    allowed = (column <= row) & (column < length)
    scores = jnp.where(allowed, scores, -jnp.inf)
    top = jnp.max(scores, axis=-1, keepdims=True)
    weights = jnp.exp(scores - top)
    return (weights / jnp.sum(weights, axis=-1, keepdims=True)).astype(BF)


def prepare_kernel(
    core, counts, starts, lengths,
    received, visual, queries, keys, down, up, gain, embeddings, cotangent,
    weights, entry, cotangent_half, downs, ups, gains, payload,
):
    own = core[0]
    other = 1 - own
    at = pl.multiple_of(own * HALF, HALF)
    key_at = pl.multiple_of(own * HD, HD)
    half = pl.ds(at, HALF)
    downs[own] = down[:, half]
    downs[other] = received[R_DN:R_UP, :]
    ups[own] = up[...]
    ups[other] = received[R_UP:R_GN, :]
    gains[own] = gain[:, half]
    gains[other] = received[R_GN:R_END, :]
    position = lax.broadcasted_iota(jnp.int32, (SEQ, VIS), 0)
    slot = lax.broadcasted_iota(jnp.int32, (SEQ, VIS), 1)
    place = lax.broadcasted_iota(jnp.int32, (SEQ, 1), 0)
    for index, table in ((own, visual[:, half]), (other, received[R_VIS:R_Q, :])):
        begin = starts[index]
        count = counts[index] * TOKT
        placing = ((position == begin + slot) & (slot < count)).astype(F32).astype(BF)
        inserted = nn(placing, table).astype(BF)
        covered = (place >= begin) & (place < begin + count)
        rows = pl.ds(pl.multiple_of(index * SEQ, SEQ), SEQ)
        entry[rows, :] = jnp.where(covered, inserted, embeddings[index, :, half])
    for m in range(MB):
        rows = slice(m * SEQ, (m + 1) * SEQ)
        cotangent_half[rows, :] = cotangent[m, :, half]
        weights[own, m] = softmax_of(queries[rows, half], keys[rows, pl.ds(key_at, HD)], lengths[m])
        other_keys = jnp.concatenate(
            [received[R_K:R_DN, j * HD : (j + 1) * HD] for j in range(4 * m, 4 * m + 4)], axis=0
        )
        weights[other, m] = softmax_of(
            received[R_Q + m * SEQ : R_Q + (m + 1) * SEQ, :], other_keys, lengths[m]
        )
    value_gradient = jnp.concatenate(
        [
            tn(weights[1, m], stack_heads(cotangent_half[m * SEQ : (m + 1) * SEQ, :]))
            for m in range(MB)
        ],
        axis=0,
    ).astype(BF)
    entry_float = entry[...].astype(F32)
    squares = jnp.sum(entry_float * entry_float, axis=-1, keepdims=True)
    gained = (entry_float * gains[0][0:1, :].astype(F32)).astype(BF)
    block = payload_block(value_gradient, squares, nt(downs[0], gained))
    for peer in range(PEERS):
        payload[peer] = block


def entry_norm_kernel(
    core, received, entry, ups, gains,
    normed, inverse, adapter_rows, full_gradient, own_gradient, lora_gradient,
):
    rows, low_rank = total_of_payloads(received)
    column = inverse_of(rows_to_columns(rows)[:, 0:1])
    inverse[...] = jnp.broadcast_to(column, (ROWS, HD))
    adapter_rows[...] = low_rank * inverse_of(rows[0:1, :])
    gain = gains[0][0:1, :].astype(F32)
    normed[...] = (entry[...].astype(F32) * column * gain).astype(BF)
    for head in range(KVH):
        full_gradient[:, head * HD : (head + 1) * HD] = received[block_of(head), :ROWS, :]
    own_gradient[...] = received[core[0] * 4 + core[1], :ROWS, :]
    lora_gradient[...] = ADAPTER_SCALE * nt(ups[1], full_gradient[...])


def values_kernel(layer, normed, columns, downs, ups, out):
    rows = normed[...]
    adapter = (ADAPTER_SCALE * nt(rows, downs[layer])).astype(BF)
    for pair in range(KVH // 2):
        weight = columns[2 * pair : 2 * pair + 2, layer].reshape(2 * HD, HALF)
        up = ups[layer][:, 2 * pair * HD : (2 * pair + 2) * HD]
        partial = (nt(rows, weight) + nn(adapter, up)).astype(BF)
        out[block_of(2 * pair)] = partial[:, :HD]
        out[block_of(2 * pair + 1)] = partial[:, HD:]


def scaled_kernel(full_gradient, lora_gradient, columns, downs, gains, scaled):
    weight = columns[:, 1].reshape(KVH * HD, HALF)
    grad = nn(full_gradient[...], weight) + tn(lora_gradient[...].astype(BF), downs[1])
    scaled[...] = grad * gains[1][0:1, :].astype(F32)


def attended_rows(weights, layer, value_rows):
    return jnp.concatenate(
        [
            unstack_heads(nn(weights[layer, m], value_rows[m * SEQ : (m + 1) * SEQ, :]))
            for m in range(MB)
        ],
        axis=0,
    )


def first_output_kernel(
    received, weights, entry, scaled, hidden, value_rows, payload
):
    values = received[0].astype(F32)
    for peer in range(1, PEERS):
        values = values + received[peer].astype(F32)
    value_rows[...] = values
    attended = attended_rows(weights, 0, values.astype(BF))
    output = (entry[...].astype(F32) + attended).astype(BF)
    hidden[...] = output
    output_float = output.astype(F32)
    squares = jnp.sum(output_float * output_float, axis=-1, keepdims=True)
    dots = jnp.sum(output_float * scaled[...], axis=-1, keepdims=True)
    block = columns_to_rows(squares, dots)
    for peer in range(PEERS):
        payload[peer] = block


def first_gradient_kernel(
    received, weights, hidden, scaled, cotangent_half, gains, downs, value_rows, lora_gradient,
    gradient, normed, kept, payload,
):
    total = received[0]
    for peer in range(1, PEERS):
        total = total + received[peer]
    sums = rows_to_columns(total)
    column = inverse_of(sums[:, 0:1])
    factor = column * column * column * sums[:, 1:2] / MODEL_WIDTH
    hidden_float = hidden[...].astype(F32)
    gained = hidden_float * gains[1][0:1, :].astype(F32)
    rows = (gained * column).astype(BF)
    normed[...] = rows
    kept[:RANK, :] = nn(lora_gradient[...].astype(BF), rows)
    kept[RANK:, :ROWS] = inverse_of(total)
    kept[RANK:, ROWS:] = jnp.zeros((SUBLANES, HALF - ROWS), F32)
    grad = (
        cotangent_half[...].astype(F32) + column * scaled[...] - hidden_float * factor
    ).astype(BF)
    gradient[...] = grad
    value_gradient = jnp.concatenate(
        [tn(weights[0, m], stack_heads(grad[m * SEQ : (m + 1) * SEQ, :])) for m in range(MB)],
        axis=0,
    ).astype(BF)
    dots = jnp.sum(value_gradient.astype(F32) * value_rows[...], axis=-1, keepdims=True)
    block = payload_block(value_gradient, dots, nt(downs[1], gained.astype(BF)))
    for peer in range(PEERS):
        payload[peer] = block


def map_chunks(down_gradient, up_gradient):
    quarter = HALF // 4
    left = jnp.concatenate(
        [down_gradient[:, q * quarter : (q + 1) * quarter] for q in range(4)], axis=0
    )
    right = jnp.concatenate([up_gradient, jnp.zeros((3 * RANK, HD), F32)], axis=0)
    return jnp.concatenate([left, right], axis=1)


def gathered_gradient(received):
    return jnp.concatenate([received[block_of(head), :ROWS, :] for head in range(KVH)], axis=1)


def map_gradient_kernel(
    core, received, ups, normed_0, adapter_0, gradient_1, kept, out
):
    _, low_rank = total_of_payloads(received)
    lora_0 = ADAPTER_SCALE * nt(ups[0], gathered_gradient(received))
    own = received[core[0] * 4 + core[1], :ROWS, :]
    down_0 = nn(lora_0.astype(BF), normed_0[...])
    up_0 = ADAPTER_SCALE * nn(adapter_0[...].astype(BF), own)
    adapter_1 = (low_rank * kept[RANK : RANK + 1, :ROWS]).astype(BF)
    up_1 = ADAPTER_SCALE * nn(adapter_1, gradient_1[...])
    chunks = (map_chunks(down_0, up_0), map_chunks(kept[:RANK, :], up_1))
    for layer in range(2):
        out[layer * 4 * RANK : (layer + 1) * 4 * RANK] = chunks[layer][:, None, :]


def slot_gradient_kernel(
    core, counts, starts, received, ups, columns, downs, gains, entry, inverse, gradient,
    own_slots, other_slots, token,
):
    token[...] = jnp.zeros_like(token)
    dots, _ = total_of_payloads(received)
    full_gradient = gathered_gradient(received)
    lora_gradient = ADAPTER_SCALE * nt(ups[0], full_gradient)
    column = inverse[:, 0:1]
    factor = column * column * rows_to_columns(dots)[:, 0:1] / MODEL_WIDTH
    weight = columns[:, 0].reshape(KVH * HD, HALF)
    grad = nn(full_gradient, weight) + tn(lora_gradient.astype(BF), downs[0])
    scaled = grad * gains[0][0:1, :].astype(F32)
    rows = (
        gradient[...].astype(F32) + column * scaled - entry[...].astype(F32) * factor
    ).astype(BF)
    slot = lax.broadcasted_iota(jnp.int32, (VIS, SEQ), 0)
    position = lax.broadcasted_iota(jnp.int32, (VIS, SEQ), 1)
    first = core[0] == 0
    above, below = rows[:SEQ, :], rows[SEQ:, :]
    for index, block, out in (
        (core[0], jnp.where(first, above, below), own_slots),
        (1 - core[0], jnp.where(first, below, above), other_slots),
    ):
        inside = (position == starts[index] + slot) & (slot < counts[index] * TOKT)
        out[...] = nn(inside.astype(F32).astype(BF), block).astype(BF)


def second_output_kernel(core, values, weights, hidden, own_hidden, other_hidden):
    attended = attended_rows(weights, 1, values[...])
    output = (hidden[...].astype(F32) + attended).astype(BF)
    first = core[0] == 0
    own_hidden[...] = jnp.where(first, hidden[...], output)
    other_hidden[...] = jnp.where(first, output, hidden[...])


def sum_kernel(arrived, out, token):
    token[...] = jnp.zeros_like(token)
    n_fsdp = arrived.shape[0] // 2
    halves = [jnp.sum(arrived[h * n_fsdp : (h + 1) * n_fsdp], axis=0) for h in range(2)]
    row = jnp.concatenate(halves, axis=1)
    for at in range(n_fsdp):
        out[at] = row


def maps_kernel(arrived, down_sum, up_sum, *, scale):
    rows = arrived[...].reshape(4 * RANK, 2 * (HALF // 4 + HD)) * scale
    quarter, width = HALF // 4, HALF // 4 + HD
    for half in range(2):
        for q in range(4):
            to = half * HALF + q * quarter
            down_sum[:, to : to + quarter] = rows[
                q * RANK : (q + 1) * RANK, half * width : half * width + quarter
            ]
        up_sum[:, half * HD : (half + 1) * HD] = rows[
            :RANK, half * width + quarter : (half + 1) * width
        ]


def place_kernel(core, own, other, out, token):
    token[...] = jnp.zeros_like(token)
    at = pl.multiple_of(core[0] * HALF, HALF)
    out[:, pl.ds(at, HALF)] = own[...]
    out[:, pl.ds(HALF - at, HALF)] = other[...]


def call(kernel, name, results, scalars, arrays, after=()):
    n_read = len(scalars) + len(arrays)

    def body(*refs):
        kernel(*refs[:n_read], *refs[n_read + len(after) :])

    moved = sum(a.size * a.dtype.itemsize for a in arrays)
    moved += sum(math.prod(shape) * jnp.dtype(dtype).itemsize for shape, dtype in results)
    in_vmem = pl.BlockSpec(memory_space=pltpu.VMEM)
    return pl.pallas_call(
        body,
        out_shape=[jax.ShapeDtypeStruct(shape, dtype) for shape, dtype in results],
        in_specs=[pl.BlockSpec(memory_space=pltpu.SMEM)] * len(scalars)
        + [in_vmem] * len(arrays)
        + [pl.BlockSpec(memory_space=pl.ANY)] * len(after),
        out_specs=[in_vmem] * len(results),
        compiler_params=pltpu.CompilerParams(vmem_limit_bytes=VMEM_BYTES),
        cost_estimate=pl.CostEstimate(flops=0, bytes_accessed=moved, transcendentals=0),
        name=name,
    )(*scalars, *arrays, *after)


def swap_cores(block):
    return lax.ppermute(block, "section", [(0, 1), (1, 0)])


def to_heads(block):
    return lax.all_to_all(block, ("section", "tp"), 0, 0)


def on_device(
    embeddings,
    visual,
    image_block_count,
    starts,
    lengths,
    queries,
    layer_key_vectors,
    input_norm_gain,
    frozen_value_weight,
    adapter_down_map,
    adapter_up_map,
    cotangent,
):
    section = lax.axis_index("section")
    tp = lax.axis_index("tp")
    n_fsdp = lax.axis_size("fsdp")
    n_y = n_fsdp // KVH
    core = jnp.stack([section, tp]).astype(jnp.int32)
    counts = image_block_count[:, 0]
    begins = starts[:, 0]
    seq_lengths = lengths[:, 0]

    shard = frozen_value_weight[0].T
    pieces = shard.reshape(shard.shape[0], 2, HALF).transpose(1, 0, 2)
    pieces = jnp.broadcast_to(pieces[:, None], (2, n_y) + pieces.shape[1:])
    pieces = pieces.reshape((2 * n_y,) + pieces.shape[2:])
    head_groups = [
        [s * n_fsdp + z * n_y + y for s in range(2) for y in range(n_y)] for z in range(KVH)
    ]
    head_columns = lax.all_to_all(
        pieces, ("section", "fsdp"), 0, 0, axis_index_groups=head_groups
    ).reshape(2, HD, HALF)
    row_groups = [[z * n_y + y for z in range(KVH)] for y in range(n_y)]
    columns = lax.all_gather(head_columns, "fsdp", axis=0, axis_index_groups=row_groups)

    own_visual = visual[0, 0]
    own_queries = queries[0].reshape(ROWS, 2 * HALF)
    own_keys = layer_key_vectors[0].reshape(ROWS, 2 * HD)
    own_down = adapter_down_map[0].T
    own_up = adapter_up_map[0]
    own_gain = jnp.broadcast_to(input_norm_gain, (RANK, 2 * HALF))
    own = (own_visual, own_queries, own_keys, own_down, own_up, own_gain)
    (packed,) = call(pack_kernel, "pack", [((R_END, HALF), BF)], (core,), own)
    received = swap_cores(packed)

    wide = ((ROWS, HALF), BF)
    small = ((RANK, ROWS), F32)
    maps = ((2, RANK, HALF), BF)
    weights, entry, cotangent_half, downs, ups, gains, payload = call(
        prepare_kernel,
        "prepare",
        [
            ((2, MB, HEADS * SEQ, SEQ), BF),
            wide,
            wide,
            maps,
            maps,
            maps,
            ((PEERS, R_PAY, HD), BF),
        ],
        (core, counts, begins, seq_lengths),
        (received, *own, embeddings, cotangent),
    )
    normed_0, inverse_0, adapter_0, full_gradient, own_gradient_1, lora_gradient_1 = call(
        entry_norm_kernel,
        "entry_norm",
        [wide, ((ROWS, HD), F32), small, wide, ((ROWS, HD), BF), small],
        (core,),
        (to_heads(payload), entry, ups, gains),
    )

    blocks = ((PEERS, ROWS, HD), BF)
    (partial_0,) = call(
        functools.partial(values_kernel, 0), "values_0", [blocks], (), (normed_0, columns, downs, ups)
    )
    (scaled_1,) = call(
        scaled_kernel,
        "scaled_1",
        [((ROWS, HALF), F32)],
        (),
        (full_gradient, lora_gradient_1, columns, downs, gains),
    )
    hidden_0, value_rows, payload = call(
        first_output_kernel,
        "first_output",
        [wide, ((ROWS, HD), F32), ((PEERS, SUBLANES, ROWS), F32)],
        (),
        (to_heads(partial_0), weights, entry, scaled_1),
    )
    gradient, normed_1, kept, payload = call(
        first_gradient_kernel,
        "first_gradient",
        [
            wide,
            wide,
            ((RANK + SUBLANES, HALF), F32),
            ((PEERS, R_PAY, HD), BF),
        ],
        (),
        (
            to_heads(payload),
            weights,
            hidden_0,
            scaled_1,
            cotangent_half,
            gains,
            downs,
            value_rows,
            lora_gradient_1,
        ),
    )
    gathered = to_heads(payload)
    (partial_1,) = call(
        functools.partial(values_kernel, 1), "values_1", [blocks], (), (normed_1, columns, downs, ups)
    )
    values_1 = lax.psum_scatter(partial_1, ("section", "tp"), scatter_dimension=0)

    (chunks,) = call(
        map_gradient_kernel,
        "map_gradient",
        [((2 * n_fsdp, 1, HALF // 4 + HD), F32)],
        (core,),
        (gathered, ups, normed_0, adapter_0, own_gradient_1, kept),
    )
    width = HALF // 4 + HD
    arrived = lax.all_to_all(chunks, ("section", "fsdp"), 0, 0)
    token = ((SUBLANES, HD), F32)
    summed, summed_token = call(
        sum_kernel, "sum_maps", [((n_fsdp, 1, 2 * width), F32), token], (), (arrived,)
    )
    everywhere = lax.all_to_all(summed, "fsdp", 0, 0)

    own_slots, other_slots, slots_token = call(
        slot_gradient_kernel,
        "slot_gradient",
        [((VIS, HALF), BF)] * 2 + [token],
        (core, counts, begins),
        (gathered, ups, columns, downs, gains, entry, inverse_0, gradient),
    )
    own_hidden, other_hidden = call(
        second_output_kernel,
        "second_output",
        [wide] * 2,
        (core,),
        (values_1, weights, hidden_0),
        after=(slots_token,),
    )
    slots, slots_placed = call(
        place_kernel,
        "place_slots",
        [((VIS, 2 * HALF), BF), token],
        (core,),
        (own_slots, swap_cores(other_slots)),
    )
    hidden, hidden_placed = call(
        place_kernel,
        "place_hidden",
        [((ROWS, 2 * HALF), BF), token],
        (core,),
        (own_hidden, swap_cores(other_hidden)),
    )
    down_sum, up_sum = call(
        functools.partial(maps_kernel, scale=1.0 / math.sqrt(MB * SEQ * n_fsdp)),
        "maps",
        [((RANK, 2 * HALF), F32), ((RANK, 2 * HD), F32)],
        (),
        (everywhere,),
        after=(slots_placed, hidden_placed),
    )
    return (
        hidden.reshape(1, MB, SEQ, 2 * HALF),
        slots[None, None],
        down_sum.T[None],
        up_sum[None],
    )


def solution(mesh):
    return jax.shard_map(
        on_device,
        mesh=mesh,
        in_specs=(
            P(None, "fsdp", "tp"),
            P("section", "fsdp", None, "tp"),
            P(None, "fsdp"),
            P(None, "fsdp"),
            P(None, "fsdp"),
            P("section", None, "fsdp", "tp"),
            P("section", None, "fsdp", "tp"),
            P("section", "tp"),
            P("section", "tp", "fsdp"),
            P("section", "tp", None),
            P("section", None, None),
            P(None, "fsdp", "tp"),
        ),
        out_specs=(
            P("section", None, "fsdp", "tp"),
            P("section", "fsdp", None, "tp"),
            P("section", "tp", None),
            P("section", None, "tp"),
        ),
        check_vma=False,
    )
```
